256 devices in a mesh: row: 16 (over y, x), col: 16 (over z, core).
Axes of the slice: x: 4, y: 4, z: 8, core: 2. Of those that a mesh axis runs over, the one named last changes fastest.
Arguments:
- kernel: float32 [20480, 20480], P('row', 'col'), may hold values from 0 to 3, as said below
- noise: float32 [20480], P('row'), may hold values from 0.3 to 1
Outputs:
- factored: float32 [20480, 20480], P('row', 'col')
The draws below stay inside these ranges and needn't reach their ends.
Inputs may be any that keep to these rules, and one draw needn't show every extreme that they name: In global order kernel is symmetric and positive semidefinite, and all its entries are positive.
All inputs are finite; a program needn't handle non-finite values.
Results may differ from the reference program's by a relative error of at most 0.0001.
Values sent between devices are 32-bit elements; how exact they have to be, the bound alone decides.
A program may use at most 128 MiB of HBM per device.

```python
import math
import jax
import jax.numpy as jnp
from jax import lax

NB = 256
KB = 5
RB = 5
ORDER = 20480
N_ROW = 16
N_COL = 16


def point_index(stored, per_group, groups):
    span = per_group * NB
    group = stored // span
    inner = stored % span
    return (inner // NB * groups + group) * NB + stored % NB


def draw_kernel(key, part):
    key = jax.random.fold_in(key, 7)
    coord_key, scale_key = jax.random.split(key)
    coords = jax.random.uniform(coord_key, (4, ORDER), jnp.float32)
    scales = jnp.exp(jax.random.uniform(scale_key, (ORDER,), jnp.float32, math.log(0.75), math.log(1.33)))
    stored = jnp.arange(ORDER, dtype=jnp.int32)
    row_points = point_index(stored, RB, N_ROW)
    col_points = point_index(stored, KB, N_COL)
    distance = jnp.zeros((ORDER, ORDER), jnp.float32)
    for axis_number in range(4):
        line = coords[axis_number]
        distance = distance + jnp.abs(line[row_points][:, None] - line[col_points][None, :])
    values = scales[row_points][:, None] * scales[col_points][None, :] * jnp.exp(-distance)
    return values.astype(jnp.float32)


def steps_of(stream_key, shape, shards, smallest, top_value):
    loudness, own = 1.0, jax.random.fold_in(stream_key, 6)
    for dim, blocks in shards:
        heights = jnp.exp(jax.random.uniform(jax.random.fold_in(own, dim), (blocks,), jnp.float32, smallest / len(shards), top_value / len(shards)))
        loudness = loudness * jnp.repeat(heights, shape[dim] // blocks).reshape([-1 if axis == dim else 1 for axis in range(len(shape))])
    return loudness


def setup_inputs(seed: int = 0) -> dict:
    key_list = jax.random.split(jax.random.key(seed), 3)
    kernel = draw_kernel(jax.random.fold_in(key_list[2], 71), 0)
    noise = jnp.clip(0.3 + 0.7 * jax.random.uniform(key_list[1], (ORDER,), jnp.float32) ** steps_of(key_list[1], (ORDER,), ((0, 16),), -0.2, 0.2), 0.3, 1.0)
    return dict(kernel=kernel, noise=noise)


def rows_global(x, parts):
    total = x.shape[0]
    per = total // NB // parts
    return x.reshape(parts, per, NB, x.shape[1]).transpose(1, 0, 2, 3).reshape(total, x.shape[1])

def rows_stored(x, parts):
    total = x.shape[0]
    per = total // NB // parts
    return x.reshape(per, parts, NB, x.shape[1]).transpose(1, 0, 2, 3).reshape(total, x.shape[1])

def factor_block(block):
    whole = jnp.tril(block) + jnp.tril(block, -1).T
    factor = jnp.linalg.cholesky(whole)
    eye = jnp.eye(block.shape[0], dtype=block.dtype)
    inverse = lax.linalg.triangular_solve(factor, eye, left_side=True, lower=True)
    return (factor, inverse)

def reference(kernel, noise):
    matrix = rows_global(kernel, N_ROW)
    matrix = rows_global(matrix.T, N_COL).T
    diag_noise = rows_global(noise[:, None], N_ROW)[:, 0]
    index = jnp.arange(ORDER)
    matrix = matrix.at[index, index].add(diag_noise)
    block_id = index // NB
    for k in range(2):
        low = k * NB
        high = low + NB
        factor, inverse = factor_block(matrix[low:high, low:high])
        panel = jnp.dot(matrix[high:, low:high].astype(jnp.float32), inverse.T.astype(jnp.float32), precision=lax.Precision.HIGHEST, preferred_element_type=jnp.float32)
        update = jnp.dot(panel.astype(jnp.float32), panel.T.astype(jnp.float32), precision=lax.Precision.HIGHEST, preferred_element_type=jnp.float32)
        rest = block_id[high:]
        keep = rest[:, None] >= rest[None, :]
        trailing = jnp.where(keep, matrix[high:, high:] - update, matrix[high:, high:])
        matrix = matrix.at[high:, high:].set(trailing)
        matrix = matrix.at[high:, low:high].set(panel)
        matrix = matrix.at[low:high, low:high].set(factor)
    matrix = rows_stored(matrix.T, N_COL).T
    return rows_stored(matrix, N_ROW)
```

```python
import functools

import jax
import jax.numpy as jnp
from jax import lax
from jax.experimental import pallas as pl
from jax.experimental.pallas import tpu as pltpu
from jax.sharding import PartitionSpec as P

NB = 256
T = 5
LOCAL = NB * T
MESH = pl.DeviceIdType.MESH
HIGHEST = lax.Precision.HIGHEST
HIGH = lax.Precision.HIGH
F32 = jnp.float32

NA = 20
A_ROWS = LOCAL // NA
NBC = 16
B_ROWS = NB // NBC
NF = 6
F_ROWS = NB * 3 // NF


def dot(a, b, dims, precision=HIGHEST):
    return lax.dot_general(a, b, (dims, ((), ())), precision=precision, preferred_element_type=F32)


def nn(a, b, precision=HIGHEST):
    return dot(a, b, ((1,), (0,)), precision)


def nt(a, b, precision=HIGHEST):
    return dot(a, b, ((1,), (1,)), precision)


def tn(a, b, precision=HIGHEST):
    return dot(a, b, ((0,), (0,)), precision)


def eliminate(rows, first):
    width = rows.shape[1]
    done = []
    for g in range(4):
        n = rows.shape[0]
        sub = lax.broadcasted_iota(jnp.int32, (n, 128), 0)
        at = first + 8 * g
        cols = [jnp.broadcast_to(rows[:, at + c : at + c + 1], (n, 128)) for c in range(8)]
        for j in range(8):
            inv = pltpu.reciprocal(cols[j][j : j + 1, :], approx=True)
            scale = jnp.where(sub > j, cols[j] * inv, 0.0)
            for c in range(j + 1, 8):
                cols[c] = cols[c] - scale * cols[c][j : j + 1, :]
            pivot = rows[j : j + 1, :]
            rows = jnp.concatenate(
                [rows[:, w : w + 128] - scale * pivot[:, w : w + 128] for w in range(0, width, 128)], axis=1
            )
        sub8 = lax.broadcasted_iota(jnp.int32, (8, 128), 0)
        diag = cols[0][:8]
        for j in range(1, 8):
            diag = jnp.where(sub8 == j, cols[j][:8], diag)
        root = lax.rsqrt(diag)
        done.append(rows[:8] * jnp.concatenate([root] * (width // 128), axis=1))
        rows = rows[8:]
    return jnp.concatenate(done, axis=0)


def factor_inverse(work):
    following = None
    for k in range(8):
        r0 = 32 * k
        lo, hi = r0 // 128 * 128, NB + (r0 + 32 + 127) // 128 * 128
        rows = work[r0 : r0 + 32, lo:hi] if following is None else following
        rows = eliminate(rows, r0 - lo)
        work[r0 : r0 + 32, lo:hi] = rows
        if k == 7:
            break
        r1 = r0 + 32
        lo1, hi1 = r1 // 128 * 128, NB + (r1 + 32 + 127) // 128 * 128
        product = tn(rows[:, r1 - lo : r1 - lo + 32], rows)
        if hi1 > hi:
            product = jnp.concatenate([product, jnp.zeros((32, hi1 - hi), F32)], axis=1)
        following = work[r1 : r1 + 32, lo1:hi1] - product[:, lo1 - lo :]
        if k < 6:
            r2 = r1 + 32
            lo2 = r2 // 128 * 128
            product = tn(rows[:, lo2 - lo : NB - lo], rows[:, lo2 - lo :])
            work[r2:NB, lo2:hi] = work[r2:NB, lo2:hi] - product[r2 - lo2 :, :]


def identity():
    i0 = lax.broadcasted_iota(jnp.int32, (NB, NB), 0)
    i1 = lax.broadcasted_iota(jnp.int32, (NB, NB), 1)
    return i0 == i1


def gather_kernel(
    kernel_ref, noise_ref, a_out, b_out, f_out,
    a_buf, b_buf, f_buf, m_buf, work,
    a_recv, a_send, s_recv, s_send, b_recv, b_send, f_recv, f_send, m_recv, m_send, local,
):
    p, q = lax.axis_index("row"), lax.axis_index("col")
    y, x, z, c = p // 4, p % 4, q // 2, q % 2
    xp, xm = y * 4 + (x + 1) % 4, y * 4 + (x + 3) % 4
    yp, ym = (y + 1) % 4 * 4 + x, (y + 3) % 4 * 4 + x
    zp, zm = (z + 1) % 8 * 2 + c, (z + 7) % 8 * 2 + c
    sib = z * 2 + 1 - c
    to_xp, to_xm, to_yp, to_ym = (xp, q), (xm, q), (yp, q), (ym, q)
    to_zp, to_zm, to_sib = (p, zp), (p, zm), (p, sib)
    head = (p == 0) & (q == 0)

    a_load = pltpu.make_async_copy(kernel_ref.at[:, pl.ds(0, NB)], a_buf.at[c], local.at[0])
    b_load = pltpu.make_async_copy(kernel_ref.at[pl.ds(0, NB), :], b_buf.at[p % 2], local.at[1])

    @pl.when(z == 0)
    def _():
        a_load.start()

    @pl.when(p < 2)
    def _():
        b_load.start()

    barrier = pltpu.get_barrier_semaphore()
    for device in (to_xp, to_xm, to_yp, to_ym, to_zp, to_zm, to_sib):
        pl.semaphore_signal(barrier, inc=1, device_id=device, device_id_type=MESH)

    @pl.when(head)
    def _():
        pl.semaphore_signal(barrier, inc=1, device_id=(1, 1), device_id_type=MESH)

    @pl.when(z == 0)
    def _():
        a_load.wait()

    @pl.when(p < 2)
    def _():
        b_load.wait()

    @pl.when((z == 0) & (p == c))
    def _():
        a_buf[c, :NB, :] = a_buf[c, :NB, :] + jnp.where(identity(), noise_ref[:, :NB], 0.0)

    pl.semaphore_wait(barrier, jnp.where((p == 1) & (q == 1), 8, 7))

    def m_copy(which):
        return pltpu.make_async_remote_copy(
            src_ref=a_buf.at[which, pl.ds(0, NB), :], dst_ref=m_buf.at[which],
            send_sem=m_send.at[which], recv_sem=m_recv.at[which], device_id=(0, 0), device_id_type=MESH,
        )

    @pl.when((p == 1) & (q == 0))
    def _():
        m_copy(0).start()

    @pl.when((p == 1) & (q == 1))
    def _():
        m_copy(1).start()

    def a_ring(n, device):
        part = a_buf.at[c, pl.ds(n * A_ROWS, A_ROWS), :]
        return pltpu.make_async_remote_copy(
            src_ref=part, dst_ref=part, send_sem=a_send.at[n], recv_sem=a_recv.at[n],
            device_id=device, device_id_type=MESH,
        )

    def a_sib(n, stream):
        part = a_buf.at[stream, pl.ds(n * A_ROWS, A_ROWS), :]
        return pltpu.make_async_remote_copy(
            src_ref=part, dst_ref=part, send_sem=s_send.at[n], recv_sem=s_recv.at[n],
            device_id=to_sib, device_id_type=MESH,
        )

    def b_copy(s, n, way, device):
        part = b_buf.at[s, pl.ds(n * B_ROWS, B_ROWS), :]
        return pltpu.make_async_remote_copy(
            src_ref=part, dst_ref=part, send_sem=b_send.at[way, s, n], recv_sem=b_recv.at[s, n],
            device_id=device, device_id_type=MESH,
        )

    def f_copy(n, way, device):
        part = f_buf.at[pl.ds(n * F_ROWS, F_ROWS), :]
        return pltpu.make_async_remote_copy(
            src_ref=part, dst_ref=part, send_sem=f_send.at[way, n], recv_sem=f_recv.at[n],
            device_id=device, device_id_type=MESH,
        )

    a_more = (z != 7, z != 1)
    a_next = (to_zp, to_zm)
    y_next = (to_yp, to_ym)

    def b_ways(s, back):
        y_more = y != (1 if back else 3)
        if s == 0:
            return (
                ((y == 0) & (x == 0), to_xp),
                ((y == 0) & ((x == 0) | (x == 3)), to_xm),
                (y_more, y_next[back]),
            )
        return (
            ((y == 0) & ((x == 1) | (x == 2)), to_xp),
            (x == 1, to_xm),
            (y_more & (x >= 1), y_next[back]),
        )

    def pump(m, carry):
        for back in range(2):
            n = 2 * m + back

            @pl.when(z != 0)
            def _():
                a_ring(n, a_next[back]).wait_recv()

            @pl.when(a_more[back])
            def _():
                a_ring(n, a_next[back]).start()

            a_sib(n, c).start()

        @pl.when(m < NBC // 2)
        def _():
            for s in range(2):
                for back in range(2):
                    n = 2 * m + back

                    @pl.when((p != s) & jnp.logical_not(head))
                    def _():
                        b_copy(s, n, 0, to_xp).wait_recv()

                    for way, (sends, device) in enumerate(b_ways(s, back)):
                        @pl.when(sends)
                        def _():
                            b_copy(s, n, way, device).start()

        return carry

    lax.fori_loop(0, NA // 2, pump, 0)

    core0 = c == 0
    f_ways = (
        (core0 & (p == 0) & (z < 4), to_zp),
        (core0 & (p == 0) & ((z == 0) | (z > 5)), to_zm),
        (core0 & (y == 0) & (x < 2), to_xp),
        (core0 & (p == 0), to_xm),
        (core0 & (y < 2), to_yp),
        (core0 & (y == 0), to_ym),
        (core0, to_sib),
    )

    def f_send_all(n):
        for way, (sends, device) in enumerate(f_ways):
            @pl.when(sends)
            def _():
                f_copy(n, way, device).start()

    @pl.when(head)
    def _():
        eye = jnp.where(identity(), 1.0, 0.0)
        work[:, :NB] = a_buf[0, :NB, :]
        work[:, NB:] = eye
        factor_inverse(work)
        f_buf[:NB, :] = work[:, NB:]
        for n in range(2):
            f_send_all(n)
        m_copy(0).wait_recv()
        f_buf[NB : 2 * NB, :] = nt(m_buf[0], f_buf[:NB, :])
        for n in range(2, 4):
            f_send_all(n)
        m_copy(1).wait_recv()
        l10 = f_buf[NB : 2 * NB, :]
        work[:, :NB] = m_buf[1] - nt(l10, l10)
        work[:, NB:] = eye
        factor_inverse(work)
        f_buf[2 * NB :, :] = work[:, NB:]
        for n in range(4, 6):
            f_send_all(n)

        def rest(n, carry):
            b_copy(1, n, 0, to_xp).wait_recv()
            return carry

        lax.fori_loop(0, NBC, rest, 0)

    @pl.when(jnp.logical_not(head))
    def _():
        def relay(n, carry):
            f_copy(n, 0, to_zp).wait_recv()
            f_send_all(n)
            return carry

        lax.fori_loop(0, NF, relay, 0)

    def finish_a(m, carry):
        for back in range(2):
            n = 2 * m + back
            a_sib(n, 1 - c).wait_recv()
            a_sib(n, c).wait_send()

            @pl.when(a_more[back])
            def _():
                a_ring(n, a_next[back]).wait_send()

        return carry

    lax.fori_loop(0, NA // 2, finish_a, 0)

    def finish_b(m, carry):
        for s in range(2):
            for back in range(2):
                n = 2 * m + back
                for way, (sends, device) in enumerate(b_ways(s, back)):
                    @pl.when(sends)
                    def _():
                        b_copy(s, n, way, device).wait_send()

        return carry

    lax.fori_loop(0, NBC // 2, finish_b, 0)

    def finish_f(n, carry):
        for way, (sends, device) in enumerate(f_ways):
            @pl.when(sends)
            def _():
                f_copy(n, way, device).wait_send()

        return carry

    lax.fori_loop(0, NF, finish_f, 0)

    @pl.when((p == 1) & (q == 0))
    def _():
        m_copy(0).wait_send()

    @pl.when((p == 1) & (q == 1))
    def _():
        m_copy(1).wait_send()

    outs = [
        pltpu.make_async_copy(a_buf, a_out, local.at[0]),
        pltpu.make_async_copy(b_buf, b_out, local.at[1]),
        pltpu.make_async_copy(f_buf, f_out, local.at[2]),
    ]
    for out in outs:
        out.start()
    for out in outs:
        out.wait()


def gather(kernel, noise):
    return pl.pallas_call(
        gather_kernel,
        out_shape=(
            jax.ShapeDtypeStruct((2, LOCAL, NB), F32),
            jax.ShapeDtypeStruct((2, NB, LOCAL), F32),
            jax.ShapeDtypeStruct((3 * NB, NB), F32),
        ),
        in_specs=[pl.BlockSpec(memory_space=pl.ANY), pl.BlockSpec(memory_space=pltpu.VMEM)],
        out_specs=[pl.BlockSpec(memory_space=pl.ANY)] * 3,
        scratch_shapes=[
            pltpu.VMEM((2, LOCAL, NB), F32),
            pltpu.VMEM((2, NB, LOCAL), F32),
            pltpu.VMEM((3 * NB, NB), F32),
            pltpu.VMEM((2, NB, NB), F32),
            pltpu.VMEM((NB, 2 * NB), F32),
            pltpu.SemaphoreType.DMA((NA,)),
            pltpu.SemaphoreType.DMA((NA,)),
            pltpu.SemaphoreType.DMA((NA,)),
            pltpu.SemaphoreType.DMA((NA,)),
            pltpu.SemaphoreType.DMA((2, NBC)),
            pltpu.SemaphoreType.DMA((3, 2, NBC)),
            pltpu.SemaphoreType.DMA((NF,)),
            pltpu.SemaphoreType.DMA((7, NF)),
            pltpu.SemaphoreType.DMA((2,)),
            pltpu.SemaphoreType.DMA((2,)),
            pltpu.SemaphoreType.DMA((3,)),
        ],
        compiler_params=pltpu.CompilerParams(
            collective_id=0, has_side_effects=True, vmem_limit_bytes=48 * 2**20
        ),
        name="gather_factor",
    )(kernel, noise)


def update_kernel(m_ref, noise_ref, a_ref, b_ref, f_ref, out_ref, cols):
    p, q = lax.axis_index("row"), lax.axis_index("col")
    t = pl.program_id(0)
    x0, l10, x1 = f_ref[:NB, :], f_ref[NB : 2 * NB, :], f_ref[2 * NB :, :]

    @pl.when(t == 0)
    def _():
        for col in range(T):
            at = slice(col * NB, (col + 1) * NB)
            col0 = nn(x0, b_ref[0, :, at])
            cols[:NB, at] = col0
            cols[NB:, at] = nn(x1, b_ref[1, :, at] - nn(l10, col0))

    row0 = nt(a_ref[0], x0)
    row1 = nt(a_ref[1] - nt(row0, l10), x1)
    rows = jnp.concatenate([row0, row1], axis=1)
    i = t * 16 + p
    i0 = lax.broadcasted_iota(jnp.int32, (NB, NB), 0)
    i1 = lax.broadcasted_iota(jnp.int32, (NB, NB), 1)
    for col in range(T):
        at = slice(col * NB, (col + 1) * NB)
        j = col * 16 + q
        panel = j < 2
        below = jnp.logical_not(panel) & (i >= j)

        @pl.when(below)
        def _():
            on_diag = (i0 == i1) & (i == j)
            block = m_ref[:, at] + jnp.where(on_diag, noise_ref[...], 0.0)
            out_ref[:, at] = block - nn(rows, cols[:, at], HIGH)

        @pl.when(panel & (i >= j))
        def _():
            value = jnp.where(q == 0, row0, row1)
            out_ref[:, at] = jnp.where((i == j) & (i0 < i1), 0.0, value)

        @pl.when(i < j)
        def _():
            out_ref[:, at] = m_ref[:, at]


def update(kernel, noise, a, b, f):
    return pl.pallas_call(
        update_kernel,
        grid=(T,),
        out_shape=jax.ShapeDtypeStruct((LOCAL, LOCAL), F32),
        in_specs=[
            pl.BlockSpec((NB, LOCAL), lambda t: (t, 0)),
            pl.BlockSpec((1, NB), lambda t: (0, t)),
            pl.BlockSpec((2, NB, NB), lambda t: (0, t, 0)),
            pl.BlockSpec((2, NB, LOCAL), lambda t: (0, 0, 0)),
            pl.BlockSpec((3 * NB, NB), lambda t: (0, 0)),
        ],
        out_specs=pl.BlockSpec((NB, LOCAL), lambda t: (t, 0)),
        scratch_shapes=[pltpu.VMEM((2 * NB, LOCAL), F32)],
        compiler_params=pltpu.CompilerParams(vmem_limit_bytes=48 * 2**20),
        name="update",
    )(kernel, noise, a, b, f)


def body(kernel, noise):
    noise = noise.reshape(1, LOCAL)
    a, b, f = gather(kernel, noise)
    return update(kernel, noise, a, b, f)


def solution(mesh):
    return jax.shard_map(
        body,
        mesh=mesh,
        in_specs=(P("row", "col"), P("row")),
        out_specs=P("row", "col"),
        check_vma=False,
    )
```

```python
import functools

import jax
import jax.numpy as jnp
from jax import lax
from jax.experimental import pallas as pl
from jax.experimental.pallas import tpu as pltpu
from jax.sharding import PartitionSpec as P

NB = 256
T = 5
LOCAL = NB * T
MESH = pl.DeviceIdType.MESH
HIGHEST = lax.Precision.HIGHEST
HIGH = lax.Precision.HIGH
F32 = jnp.float32

NA = 20
A_ROWS = LOCAL // NA
NBC = 32
B_ROWS = NB // NBC
PIECES = ((0, 256), (256, 256), (512, 128), (640, 64), (704, 32), (736, 32))
NF = len(PIECES)
SLOTS = 24


def dot(a, b, dims, precision=HIGHEST):
    return lax.dot_general(a, b, (dims, ((), ())), precision=precision, preferred_element_type=F32)


def nn(a, b, precision=HIGHEST):
    return dot(a, b, ((1,), (0,)), precision)


def nt(a, b, precision=HIGHEST):
    return dot(a, b, ((1,), (1,)), precision)


def tn(a, b, precision=HIGHEST):
    return dot(a, b, ((0,), (0,)), precision)


def eliminate(rows, first):
    width = rows.shape[1]
    done = []
    for g in range(4):
        n = rows.shape[0]
        sub = lax.broadcasted_iota(jnp.int32, (n, 128), 0)
        at = first + 8 * g
        cols = [jnp.broadcast_to(rows[:, at + c : at + c + 1], (n, 128)) for c in range(8)]
        for j in range(8):
            inv = pltpu.reciprocal(cols[j][j : j + 1, :], approx=True)
            scale = jnp.where(sub > j, cols[j] * inv, 0.0)
            for c in range(j + 1, 8):
                cols[c] = cols[c] - scale * cols[c][j : j + 1, :]
            pivot = rows[j : j + 1, :]
            rows = jnp.concatenate(
                [rows[:, w : w + 128] - scale * pivot[:, w : w + 128] for w in range(0, width, 128)], axis=1
            )
        sub8 = lax.broadcasted_iota(jnp.int32, (8, 128), 0)
        diag = cols[0][:8]
        for j in range(1, 8):
            diag = jnp.where(sub8 == j, cols[j][:8], diag)
        root = lax.rsqrt(diag)
        done.append(rows[:8] * jnp.concatenate([root] * (width // 128), axis=1))
        rows = rows[8:]
    return jnp.concatenate(done, axis=0)


def factor_inverse(work, done=lambda k: None):
    following = None
    for k in range(8):
        r0 = 32 * k
        lo, hi = r0 // 128 * 128, NB + (r0 + 32 + 127) // 128 * 128
        rows = work[r0 : r0 + 32, lo:hi] if following is None else following
        rows = eliminate(rows, r0 - lo)
        work[r0 : r0 + 32, lo:hi] = rows
        done(k)
        if k == 7:
            break
        r1 = r0 + 32
        lo1, hi1 = r1 // 128 * 128, NB + (r1 + 32 + 127) // 128 * 128
        product = tn(rows[:, r1 - lo : r1 - lo + 32], rows)
        if hi1 > hi:
            product = jnp.concatenate([product, jnp.zeros((32, hi1 - hi), F32)], axis=1)
        following = work[r1 : r1 + 32, lo1:hi1] - product[:, lo1 - lo :]
        if k < 6:
            r2 = r1 + 32
            lo2 = r2 // 128 * 128
            product = tn(rows[:, lo2 - lo : NB - lo], rows[:, lo2 - lo :])
            work[r2:NB, lo2:hi] = work[r2:NB, lo2:hi] - product[r2 - lo2 :, :]


def identity():
    i0 = lax.broadcasted_iota(jnp.int32, (NB, NB), 0)
    i1 = lax.broadcasted_iota(jnp.int32, (NB, NB), 1)
    return i0 == i1


def gather_kernel(
    kernel_ref, noise_ref, a_out, b_out, f_out,
    a_buf, b_buf, f_buf, m_buf, work,
    a_recv, a_send, s_recv, s_send, b_recv, b_send, f_recv, f_send, m_recv, m_send, local,
):
    p, q = lax.axis_index("row"), lax.axis_index("col")
    y, x, z, c = p // 4, p % 4, q // 2, q % 2
    xp, xm = y * 4 + (x + 1) % 4, y * 4 + (x + 3) % 4
    yp, ym = (y + 1) % 4 * 4 + x, (y + 3) % 4 * 4 + x
    zp, zm = (z + 1) % 8 * 2 + c, (z + 7) % 8 * 2 + c
    sib = z * 2 + 1 - c
    to_xp, to_xm, to_yp, to_ym = (xp, q), (xm, q), (yp, q), (ym, q)
    to_zp, to_zm, to_sib = (p, zp), (p, zm), (p, sib)
    head = (p == 0) & (q == 0)

    a_load = pltpu.make_async_copy(kernel_ref.at[:, pl.ds(0, NB)], a_buf.at[c], local.at[0])
    b_load = pltpu.make_async_copy(kernel_ref.at[pl.ds(0, NB), :], b_buf.at[p % 2], local.at[1])

    @pl.when(z == 0)
    def _():
        a_load.start()

    @pl.when(p < 2)
    def _():
        b_load.start()

    barrier = pltpu.get_barrier_semaphore()

    def greet(device):
        pl.semaphore_signal(barrier, inc=1, device_id=device, device_id_type=MESH)

    for device in (to_xp, to_xm, to_yp, to_ym, to_zp, to_zm, to_sib):
        greet(device)

    core0 = c == 0
    top = core0 & (p == 0)
    edge = core0 & (y == 0)

    @pl.when(head)
    def _():
        for k in range(2, 7):
            greet((0, 2 * k))
        greet((1, 1))

    @pl.when(((p == 1) & (q == 1)) | (top & (z >= 2) & (z <= 6)))
    def _():
        greet((0, 0))

    @pl.when(edge & ((x == 0) | (x == 2)))
    def _():
        greet((2 - x, q))

    @pl.when(core0 & ((y == 0) | (y == 2)))
    def _():
        greet((4 * (2 - y) + x, q))

    peers = 7 + jnp.where(head, 6, 0)
    peers += jnp.where(((p == 1) & (q == 1)) | (top & (z >= 2) & (z <= 6)), 1, 0)
    peers += jnp.where(edge & ((x == 0) | (x == 2)), 1, 0)
    peers += jnp.where(core0 & ((y == 0) | (y == 2)), 1, 0)

    @pl.when(z == 0)
    def _():
        a_load.wait()

    @pl.when(p < 2)
    def _():
        b_load.wait()

    @pl.when((z == 0) & (p == c))
    def _():
        a_buf[c, :NB, :] = a_buf[c, :NB, :] + jnp.where(identity(), noise_ref[:, :NB], 0.0)

    pl.semaphore_wait(barrier, peers)

    def m_copy(which):
        return pltpu.make_async_remote_copy(
            src_ref=a_buf.at[which, pl.ds(0, NB), :], dst_ref=m_buf.at[which],
            send_sem=m_send.at[which], recv_sem=m_recv.at[which], device_id=(0, 0), device_id_type=MESH,
        )

    @pl.when((p == 1) & (q == 0))
    def _():
        m_copy(0).start()

    @pl.when((p == 1) & (q == 1))
    def _():
        m_copy(1).start()

    def a_ring(n, device):
        part = a_buf.at[c, pl.ds(n * A_ROWS, A_ROWS), :]
        return pltpu.make_async_remote_copy(
            src_ref=part, dst_ref=part, send_sem=a_send.at[n], recv_sem=a_recv.at[n],
            device_id=device, device_id_type=MESH,
        )

    def a_sib(n, stream):
        part = a_buf.at[stream, pl.ds(n * A_ROWS, A_ROWS), :]
        return pltpu.make_async_remote_copy(
            src_ref=part, dst_ref=part, send_sem=s_send.at[n], recv_sem=s_recv.at[n],
            device_id=to_sib, device_id_type=MESH,
        )

    def b_copy(s, n, way, device):
        part = b_buf.at[s, pl.ds(n * B_ROWS, B_ROWS), :]
        return pltpu.make_async_remote_copy(
            src_ref=part, dst_ref=part, send_sem=b_send.at[way, s, n], recv_sem=b_recv.at[s, n],
            device_id=device, device_id_type=MESH,
        )

    def f_copy(n, way, device):
        part = f_buf.at[pl.ds(*PIECES[n]), :]
        return pltpu.make_async_remote_copy(
            src_ref=part, dst_ref=part, send_sem=f_send.at[way, n], recv_sem=f_recv.at[n],
            device_id=device, device_id_type=MESH,
        )

    a_more = (z != 7, z != 1)
    a_next = (to_zp, to_zm)
    a_hops = (z, (8 - z) % 8)
    plane = (to_xp, to_yp, to_xm, to_ym)

    def tree(s, k):
        dx, dy = (x + 4 - s) % 4, y
        u, v = ((dx, dy), (dy, (4 - dx) % 4), ((4 - dx) % 4, (4 - dy) % 4), ((4 - dy) % 4, dx))[k]
        side = jnp.minimum(v, 4 - v)
        hops = jnp.where((u == 0) & (v == 0), 0, jnp.where(u == 0, 2, u) + side)
        sends = (
            (u == 2) | ((u == 1) & (v < 3)) | ((u == 0) & (v == 0)),
            (u == 1) & (v < 2),
            (u == 1) & (v >= 1),
            (v == 0) & ((u == 1) | (u == 2)),
        )
        return hops, [sends[(d - k) % 4] for d in range(4)]

    def b_tree(s, k):
        hops, sends = tree(s, k)
        if (s, k) == (1, 2):
            hops0, sends0 = tree(1, 0)
            hops = jnp.where(q == 0, hops0, hops)
            sends = [((q == 0) & a) | ((q != 0) & b) for a, b in zip(sends0, sends)]
        return hops, sends

    trees = {(s, k): b_tree(s, k) for s in range(2) for k in range(4)}

    def pump(slot, carry):
        for back in range(2):
            m = slot - 2 * a_hops[back]
            n = 2 * m + back

            @pl.when((m >= 0) & (m < NA // 2))
            def _():
                @pl.when(z != 0)
                def _():
                    a_ring(n, a_next[back]).wait_recv()

                @pl.when(a_more[back])
                def _():
                    a_ring(n, a_next[back]).start()

                a_sib(n, c).start()

        for (s, k), (hops, sends) in trees.items():
            m = slot - 2 * hops
            n = 4 * m + k

            @pl.when((m >= 0) & (m < NBC // 4))
            def _():
                @pl.when((p != s) & jnp.logical_not(head))
                def _():
                    b_copy(s, n, 0, to_xp).wait_recv()

                for way in range(4):
                    @pl.when(sends[way])
                    def _():
                        b_copy(s, n, way, plane[way]).start()

        return carry

    lax.fori_loop(0, SLOTS, pump, 0)

    f_ways = [(head, (0, 2 * k)) for k in (4, 3, 5, 2, 6, 1, 7)]
    f_ways += [(top, (k, q)) for k in (2, 1, 3)]
    f_ways += [(edge, (4 * k + x, q)) for k in (2, 1, 3)]
    f_ways += [(core0, to_sib)]

    def f_send_all(n):
        for way, (sends, device) in enumerate(f_ways):
            @pl.when(sends)
            def _():
                f_copy(n, way, device).start()

    @pl.when(head)
    def _():
        eye = jnp.where(identity(), 1.0, 0.0)
        work[:, :NB] = a_buf[0, :NB, :]
        work[:, NB:] = eye
        factor_inverse(work)
        f_buf[:NB, :] = work[:, NB:]
        f_send_all(0)
        m_copy(0).wait_recv()
        l10 = nt(m_buf[0], work[:, NB:])
        f_buf[NB : 2 * NB, :] = l10
        f_send_all(1)
        m_copy(1).wait_recv()
        work[:, :NB] = m_buf[1] - nt(l10, l10)
        work[:, NB:] = eye

        def strip(k):
            last = 32 * (k + 1)
            for n in range(2, NF):
                start, size = PIECES[n]
                if start - 2 * NB + size == last:
                    f_buf[start : start + size, :] = work[last - size : last, NB:]
                    f_send_all(n)

        factor_inverse(work, strip)

        def rest(n, carry):
            b_copy(1, n, 0, to_xp).wait_recv()
            return carry

        lax.fori_loop(0, NBC, rest, 0)

    @pl.when(jnp.logical_not(head))
    def _():
        for n in range(NF):
            f_copy(n, 0, to_zp).wait_recv()
            f_send_all(n)

    def finish_a(m, carry):
        for back in range(2):
            n = 2 * m + back
            a_sib(n, 1 - c).wait_recv()
            a_sib(n, c).wait_send()

            @pl.when(a_more[back])
            def _():
                a_ring(n, a_next[back]).wait_send()

        return carry

    lax.fori_loop(0, NA // 2, finish_a, 0)

    def finish_b(m, carry):
        for (s, k), (hops, sends) in trees.items():
            for way in range(4):
                @pl.when(sends[way])
                def _():
                    b_copy(s, 4 * m + k, way, plane[way]).wait_send()

        return carry

    lax.fori_loop(0, NBC // 4, finish_b, 0)

    for n in range(NF):
        for way, (sends, device) in enumerate(f_ways):
            @pl.when(sends)
            def _():
                f_copy(n, way, device).wait_send()

    @pl.when((p == 1) & (q == 0))
    def _():
        m_copy(0).wait_send()

    @pl.when((p == 1) & (q == 1))
    def _():
        m_copy(1).wait_send()

    outs = [
        pltpu.make_async_copy(a_buf, a_out, local.at[0]),
        pltpu.make_async_copy(b_buf, b_out, local.at[1]),
        pltpu.make_async_copy(f_buf, f_out, local.at[2]),
    ]
    for out in outs:
        out.start()
    for out in outs:
        out.wait()


def gather(kernel, noise):
    return pl.pallas_call(
        gather_kernel,
        out_shape=(
            jax.ShapeDtypeStruct((2, LOCAL, NB), F32),
            jax.ShapeDtypeStruct((2, NB, LOCAL), F32),
            jax.ShapeDtypeStruct((3 * NB, NB), F32),
        ),
        in_specs=[pl.BlockSpec(memory_space=pl.ANY), pl.BlockSpec(memory_space=pltpu.VMEM)],
        out_specs=[pl.BlockSpec(memory_space=pl.ANY)] * 3,
        scratch_shapes=[
            pltpu.VMEM((2, LOCAL, NB), F32),
            pltpu.VMEM((2, NB, LOCAL), F32),
            pltpu.VMEM((3 * NB, NB), F32),
            pltpu.VMEM((2, NB, NB), F32),
            pltpu.VMEM((NB, 2 * NB), F32),
            pltpu.SemaphoreType.DMA((NA,)),
            pltpu.SemaphoreType.DMA((NA,)),
            pltpu.SemaphoreType.DMA((NA,)),
            pltpu.SemaphoreType.DMA((NA,)),
            pltpu.SemaphoreType.DMA((2, NBC)),
            pltpu.SemaphoreType.DMA((4, 2, NBC)),
            pltpu.SemaphoreType.DMA((NF,)),
            pltpu.SemaphoreType.DMA((14, NF)),
            pltpu.SemaphoreType.DMA((2,)),
            pltpu.SemaphoreType.DMA((2,)),
            pltpu.SemaphoreType.DMA((3,)),
        ],
        compiler_params=pltpu.CompilerParams(
            collective_id=0, has_side_effects=True, vmem_limit_bytes=48 * 2**20
        ),
        name="gather_factor",
    )(kernel, noise)


def split(value):
    high = value.astype(jnp.bfloat16)
    return high, (value - high.astype(F32)).astype(jnp.bfloat16)


def three(a, b, dims):
    def one(u, v):
        return lax.dot_general(u, v, (dims, ((), ())), preferred_element_type=F32)

    return one(a[0], b[0]) + (one(a[0], b[1]) + one(a[1], b[0]))


NN = ((1,), (0,))
NT = ((1,), (1,))


def update_kernel(m_ref, noise_ref, a_ref, b_ref, f_ref, out_ref, cols_high, cols_low, f_high, f_low):
    p, q = lax.axis_index("row"), lax.axis_index("col")
    t = pl.program_id(0)

    @pl.when(t == 0)
    def _():
        f_high[...], f_low[...] = split(f_ref[...])

    x0, l10, x1 = [(f_high[k * NB : (k + 1) * NB, :], f_low[k * NB : (k + 1) * NB, :]) for k in range(3)]

    @pl.when(t == 0)
    def _():
        for col in range(T):
            at = slice(col * NB, (col + 1) * NB)
            col0 = split(three(x0, split(b_ref[0, :, at]), NN))
            col1 = split(three(x1, split(b_ref[1, :, at] - three(l10, col0, NN)), NN))
            for half, value in enumerate((col0, col1)):
                cols_high[half * NB : (half + 1) * NB, at] = value[0]
                cols_low[half * NB : (half + 1) * NB, at] = value[1]

    row0 = three(split(a_ref[0]), x0, NT)
    row0_parts = split(row0)
    row1 = three(split(a_ref[1] - three(row0_parts, l10, NT)), x1, NT)
    row1_parts = split(row1)
    rows = [jnp.concatenate([u, v], axis=1) for u, v in zip(row0_parts, row1_parts)]
    i = t * 16 + p
    i0 = lax.broadcasted_iota(jnp.int32, (NB, NB), 0)
    i1 = lax.broadcasted_iota(jnp.int32, (NB, NB), 1)
    for col in range(T):
        at = slice(col * NB, (col + 1) * NB)
        j = col * 16 + q
        panel = j < 2
        below = jnp.logical_not(panel) & (i >= j)

        @pl.when(below)
        def _():
            on_diag = (i0 == i1) & (i == j)
            block = m_ref[:, at] + jnp.where(on_diag, noise_ref[...], 0.0)
            out_ref[:, at] = block - three(rows, (cols_high[:, at], cols_low[:, at]), NN)

        @pl.when(panel & (i >= j))
        def _():
            value = jnp.where(q == 0, row0, row1)
            out_ref[:, at] = jnp.where((i == j) & (i0 < i1), 0.0, value)

        @pl.when(i < j)
        def _():
            out_ref[:, at] = m_ref[:, at]


def update(kernel, noise, a, b, f):
    return pl.pallas_call(
        update_kernel,
        grid=(T,),
        out_shape=jax.ShapeDtypeStruct((LOCAL, LOCAL), F32),
        in_specs=[
            pl.BlockSpec((NB, LOCAL), lambda t: (t, 0)),
            pl.BlockSpec((1, NB), lambda t: (0, t)),
            pl.BlockSpec((2, NB, NB), lambda t: (0, t, 0)),
            pl.BlockSpec((2, NB, LOCAL), lambda t: (0, 0, 0)),
            pl.BlockSpec((3 * NB, NB), lambda t: (0, 0)),
        ],
        out_specs=pl.BlockSpec((NB, LOCAL), lambda t: (t, 0)),
        scratch_shapes=[
            pltpu.VMEM((2 * NB, LOCAL), jnp.bfloat16),
            pltpu.VMEM((2 * NB, LOCAL), jnp.bfloat16),
            pltpu.VMEM((3 * NB, NB), jnp.bfloat16),
            pltpu.VMEM((3 * NB, NB), jnp.bfloat16),
        ],
        compiler_params=pltpu.CompilerParams(vmem_limit_bytes=48 * 2**20),
        name="update",
    )(kernel, noise, a, b, f)


def body(kernel, noise):
    noise = noise.reshape(1, LOCAL)
    a, b, f = gather(kernel, noise)
    return update(kernel, noise, a, b, f)


def solution(mesh):
    return jax.shard_map(
        body,
        mesh=mesh,
        in_specs=(P("row", "col"), P("row")),
        out_specs=P("row", "col"),
        check_vma=False,
    )
```

```python
import functools

import jax
import jax.numpy as jnp
from jax import lax
from jax.experimental import pallas as pl
from jax.experimental.pallas import tpu as pltpu
from jax.sharding import PartitionSpec as P

NB = 256
T = 5
LOCAL = NB * T
MESH = pl.DeviceIdType.MESH
HIGHEST = lax.Precision.HIGHEST
HIGH = lax.Precision.HIGH
F32 = jnp.float32

NA = 20
A_ROWS = LOCAL // NA
A_SLOTS = 24
NBC = 16
B_ROWS = NB // NBC
B_SLOTS = 9
PIECES = tuple((64 * n, 64) for n in range(11)) + ((704, 32), (736, 32))
NF = len(PIECES)


def dot(a, b, dims, precision=HIGHEST):
    return lax.dot_general(a, b, (dims, ((), ())), precision=precision, preferred_element_type=F32)


def nn(a, b, precision=HIGHEST):
    return dot(a, b, ((1,), (0,)), precision)


def nt(a, b, precision=HIGHEST):
    return dot(a, b, ((1,), (1,)), precision)


def tn(a, b, precision=HIGHEST):
    return dot(a, b, ((0,), (0,)), precision)


def eliminate(rows, first):
    width = rows.shape[1]
    done = []
    for g in range(4):
        n = rows.shape[0]
        sub = lax.broadcasted_iota(jnp.int32, (n, 128), 0)
        at = first + 8 * g
        cols = [jnp.broadcast_to(rows[:, at + c : at + c + 1], (n, 128)) for c in range(8)]
        for j in range(8):
            inv = pltpu.reciprocal(cols[j][j : j + 1, :], approx=True)
            scale = jnp.where(sub > j, cols[j] * inv, 0.0)
            for c in range(j + 1, 8):
                cols[c] = cols[c] - scale * cols[c][j : j + 1, :]
            pivot = rows[j : j + 1, :]
            rows = jnp.concatenate(
                [rows[:, w : w + 128] - scale * pivot[:, w : w + 128] for w in range(0, width, 128)], axis=1
            )
        sub8 = lax.broadcasted_iota(jnp.int32, (8, 128), 0)
        diag = cols[0][:8]
        for j in range(1, 8):
            diag = jnp.where(sub8 == j, cols[j][:8], diag)
        root = lax.rsqrt(diag)
        done.append(rows[:8] * jnp.concatenate([root] * (width // 128), axis=1))
        rows = rows[8:]
    return jnp.concatenate(done, axis=0)


def factor_inverse(work, done=lambda k: None):
    following = None
    for k in range(8):
        r0 = 32 * k
        lo, hi = r0 // 128 * 128, NB + (r0 + 32 + 127) // 128 * 128
        rows = work[r0 : r0 + 32, lo:hi] if following is None else following
        rows = eliminate(rows, r0 - lo)
        work[r0 : r0 + 32, lo:hi] = rows
        done(k)
        if k == 7:
            break
        r1 = r0 + 32
        lo1, hi1 = r1 // 128 * 128, NB + (r1 + 32 + 127) // 128 * 128
        product = tn(rows[:, r1 - lo : r1 - lo + 32], rows)
        if hi1 > hi:
            product = jnp.concatenate([product, jnp.zeros((32, hi1 - hi), F32)], axis=1)
        following = work[r1 : r1 + 32, lo1:hi1] - product[:, lo1 - lo :]
        if k < 6:
            r2 = r1 + 32
            lo2 = r2 // 128 * 128
            product = tn(rows[:, lo2 - lo : NB - lo], rows[:, lo2 - lo :])
            work[r2:NB, lo2:hi] = work[r2:NB, lo2:hi] - product[r2 - lo2 :, :]


def identity():
    i0 = lax.broadcasted_iota(jnp.int32, (NB, NB), 0)
    i1 = lax.broadcasted_iota(jnp.int32, (NB, NB), 1)
    return i0 == i1


def gather_kernel(
    kernel_ref, noise_ref, a_out, b_out, f_out,
    a_buf, b_buf, f_buf, m_buf, work,
    a_recv, a_send, s_recv, s_send, b_recv, b_send, f_recv, f_send, m_recv, m_send, local,
):
    p, q = lax.axis_index("row"), lax.axis_index("col")
    y, x, z, c = p // 4, p % 4, q // 2, q % 2
    rows_next = (y * 4 + (x + 1) % 4, (y + 1) % 4 * 4 + x, y * 4 + (x + 3) % 4, (y + 3) % 4 * 4 + x)
    z_next = ((z + 1) % 8, (z + 7) % 8)
    sib = (p, z * 2 + 1 - c)
    core0, core1 = c == 0, c == 1
    head = (p == 0) & (q == 0)
    a_source, b_source = z == 0, p < 2

    def a_load(s):
        return pltpu.make_async_copy(kernel_ref.at[:, pl.ds(0, NB)], a_buf.at[s], local.at[0])

    def b_load(g, s):
        return pltpu.make_async_copy(kernel_ref.at[pl.ds(0, NB), :], b_buf.at[2 * g + s], local.at[1])

    def each_source(run_a, run_b):
        for s in range(2):
            @pl.when(a_source & (c == s))
            def _():
                run_a(s)

            for g in range(2):
                @pl.when((p == s) & (c == g))
                def _():
                    run_b(g, s)


    each_source(lambda s: a_load(s).start(), lambda g, s: b_load(g, s).start())

    barrier = pltpu.get_barrier_semaphore()
    peers = jnp.int32(7)

    def greet(device):
        pl.semaphore_signal(barrier, inc=1, device_id=device, device_id_type=MESH)

    for row in rows_next:
        greet((row, q))
    for level in z_next:
        greet((p, level * 2 + c))
    greet(sib)

    def greet_if(condition, devices):
        @pl.when(condition)
        def _():
            for device in devices:
                greet(device)

        return jnp.where(condition, len(devices), 0)

    peers += greet_if(a_source & core1, [(p, 2), (p, 14)])
    peers += greet_if(core0 & ((z == 1) | (z == 7)), [(p, 1)])
    peers += greet_if(b_source & core0, [(row, z * 2 + 1) for row in rows_next])
    for s in range(2):
        beside = ((y == 0) & ((x + 4 - s) % 2 == 1)) | ((x == s) & (y % 2 == 1))
        peers += greet_if(core1 & beside, [(s, z * 2)])
    peers += greet_if(head, [(0, 5), (0, 13)])
    peers += greet_if((p == 0) & ((q == 5) | (q == 13)), [(0, 0)])
    peers += greet_if((p == 0) & (q == 5), [(0, 9)])
    peers += greet_if((p == 0) & (q == 9), [(0, 5)])
    peers += greet_if(core1 & (y == 0) & (x % 2 == 0), [((x + 2) % 4, q)])
    peers += greet_if(core1 & (y % 2 == 0), [((y + 2) % 4 * 4 + x, q)])

    each_source(lambda s: a_load(s).wait(), lambda g, s: b_load(g, s).wait())
    for s in range(2):
        @pl.when((p == s) & (q == s))
        def _():
            a_buf[s, :NB, :] = a_buf[s, :NB, :] + jnp.where(identity(), noise_ref[:, :NB], 0.0)

    pl.semaphore_wait(barrier, peers)

    def remote(src, dst, send_sem, recv_sem, device):
        return pltpu.make_async_remote_copy(
            src_ref=src, dst_ref=dst, send_sem=send_sem, recv_sem=recv_sem, device_id=device, device_id_type=MESH
        )

    def m_copy(which):
        return remote(a_buf.at[which, pl.ds(0, NB), :], m_buf.at[which], m_send.at[which], m_recv.at[which], (0, 0))

    for which in range(2):
        @pl.when((p == 1) & (q == which))
        def _():
            m_copy(which).start()

    def a_ring(s, n, back):
        part = a_buf.at[s, pl.ds(n * A_ROWS, A_ROWS), :]
        return remote(part, part, a_send.at[s, n], a_recv.at[s, n], (p, z_next[back] * 2))

    def a_sib(s, n):
        part = a_buf.at[s, pl.ds(n * A_ROWS, A_ROWS), :]
        return remote(part, part, s_send.at[s, n], s_recv.at[s, n], sib)

    def b_plane(g, s, n, way):
        part = b_buf.at[2 * g + s, pl.ds(n * B_ROWS, B_ROWS), :]
        return remote(part, part, b_send.at[way, 2 * g + s, n], b_recv.at[2 * g + s, n], (rows_next[way], z * 2 + 1))

    def b_sib(s, n):
        part = b_buf.at[s, pl.ds(n * B_ROWS, B_ROWS), :]
        return remote(part, part, b_send.at[4, s, n], b_recv.at[s, n], sib)

    a_more = (z != 7, z != 1)
    a_hops = (z, 8 - z)

    def tree(s, k):
        dx, dy = (x + 4 - s) % 4, y
        u, v = ((dx, dy), (dy, (4 - dx) % 4), ((4 - dx) % 4, (4 - dy) % 4), ((4 - dy) % 4, dx))[k]
        hops = jnp.where(u == 0, 2, u) + jnp.minimum(v, 4 - v)
        sends = (
            (u == 2) | ((u == 1) & (v < 3)),
            (u == 1) & (v < 2),
            (u == 1) & (v >= 1),
            (v == 0) & ((u == 1) | (u == 2)),
        )
        return hops, [sends[(d - k) % 4] for d in range(4)]

    trees = {(s, k): tree(s, k) for s in range(2) for k in range(4)}

    def source(m, carry):
        def a_start(s):
            for n in range(4):
                a_ring(s, 4 * m + n, n % 2).start()
                a_sib(s, 4 * m + n).start()

        def b_start(g, s):
            for k in range(4):
                b_plane(g, s, 4 * m + k, k).start()

        each_source(a_start, b_start)
        return carry

    lax.fori_loop(0, NBC // 4, source, 0)
    for s in range(2):
        @pl.when(a_source & (c == s))
        def _():
            for n in range(NBC, NA):
                a_ring(s, n, n % 2).start()
                a_sib(s, n).start()

    def pass_a(slot, carry):
        @pl.when(core0 & (z != 0))
        def _():
            for back in range(2):
                m = slot - 2 * a_hops[back]
                n = 2 * ((m + NA) % (NA // 2)) + back

                @pl.when((m >= 0) & (m < NA // 2))
                def _():
                    for s in range(2):
                        a_ring(s, n, back).wait_recv()

                        @pl.when(a_more[back])
                        def _():
                            a_ring(s, n, back).start()

                        a_sib(s, n).start()

        return carry

    def pass_b(slot, carry):
        @pl.when(core1)
        def _():
            for (s, k), (hops, sends) in trees.items():
                m = slot - hops
                n = 4 * ((m + NBC) % (NBC // 4)) + k

                @pl.when((p != s) & (m >= 0) & (m < NBC // 4))
                def _():
                    for g in range(2):
                        b_plane(g, s, n, 0).wait_recv()
                        for way in range(4):
                            @pl.when(sends[way])
                            def _():
                                b_plane(g, s, n, way).start()

                    b_sib(s, n).start()

        return carry

    lax.fori_loop(0, A_SLOTS, pass_a, 0)
    lax.fori_loop(0, B_SLOTS, pass_b, 0)

    def a_wait_sib(s):
        def wait(n, carry):
            a_sib(s, n).wait_recv()
            return carry

        lax.fori_loop(0, NA, wait, 0)

    def b_wait_sib(n, carry):
        for s in range(2):
            @pl.when(p != s)
            def _():
                b_sib(s, n).wait_recv()

        return carry

    top = core1 & (p == 0)
    edge = core1 & (y == 0)
    f_ways = [(head, (0, 5)), (head, (0, 13)), (head, (0, 1))]
    f_ways += [(top & (z == 2), (0, k)) for k in (9, 7, 3)] + [(top & (z == 6), (0, k)) for k in (11, 15)]
    f_ways += [(top, (k, q)) for k in (2, 1, 3)]
    f_ways += [(edge, (4 * k + x, q)) for k in (2, 1, 3)]
    f_ways += [(core1 & ((p != 0) | (q != 1)), sib)]
    F_HEAD = 3

    def f_copy(n, way, device):
        part = f_buf.at[pl.ds(*PIECES[n]), :]
        return remote(part, part, f_send.at[way, n], f_recv.at[n], device)

    a_store = pltpu.make_async_copy(a_buf, a_out, local.at[0])

    def b_store(g):
        return pltpu.make_async_copy(b_buf.at[pl.ds(2 * g, 2)], b_out, local.at[1])

    f_store = pltpu.make_async_copy(f_buf, f_out, local.at[2])

    @pl.when(head)
    def _():
        eye = jnp.where(identity(), 1.0, 0.0)

        def put(first, last, value):
            f_buf[first:last, :] = value
            for n in range(NF):
                if first <= PIECES[n][0] < last:
                    for way in range(F_HEAD):
                        f_copy(n, way, f_ways[way][1]).start()

        work[:, :NB] = a_buf[0, :NB, :]
        work[:, NB:] = eye
        factor_inverse(work)
        put(0, NB, work[:, NB:])
        m_copy(0).wait_recv()
        l10 = nt(m_buf[0], work[:, NB:])
        put(NB, 2 * NB, l10)
        m_copy(1).wait_recv()
        work[:, :NB] = m_buf[1] - nt(l10, l10)
        work[:, NB:] = eye

        def strip(k):
            last = 32 * (k + 1)
            for start, size in PIECES:
                if start - 2 * NB + size == last:
                    put(start, start + size, work[last - size : last, NB:])

        factor_inverse(work, strip)
        a_wait_sib(1)
        lax.fori_loop(0, NBC, b_wait_sib, 0)
        a_store.start()
        b_store(0).start()

    @pl.when(core0 & jnp.logical_not(head))
    def _():
        @pl.when(z == 0)
        def _():
            a_wait_sib(1)

        a_store.start()
        lax.fori_loop(0, NBC, b_wait_sib, 0)
        b_store(0).start()
        for n in range(NF):
            f_copy(n, 0, sib).wait_recv()

    @pl.when(core1)
    def _():
        b_store(1).start()
        for n in range(NF):
            f_copy(n, 0, sib).wait_recv()
            for way in range(F_HEAD, len(f_ways)):
                @pl.when(f_ways[way][0])
                def _():
                    f_copy(n, way, f_ways[way][1]).start()

        a_wait_sib(0)

        @pl.when(z != 0)
        def _():
            a_wait_sib(1)

        a_store.start()

    f_store.start()

    def finish_a(m, carry):
        for back in range(2):
            n = 2 * m + back
            for s in range(2):
                @pl.when((a_source & (c == s)) | (core0 & (z != 0)))
                def _():
                    a_sib(s, n).wait_send()

                    @pl.when(a_more[back])
                    def _():
                        a_ring(s, n, back).wait_send()

        return carry

    lax.fori_loop(0, NA // 2, finish_a, 0)

    def finish_b(m, carry):
        for s in range(2):
            for g in range(2):
                @pl.when((p == s) & (c == g))
                def _():
                    for k in range(4):
                        b_plane(g, s, 4 * m + k, k).wait_send()

        @pl.when(core1)
        def _():
            for (s, k), (hops, sends) in trees.items():
                @pl.when(p != s)
                def _():
                    for g in range(2):
                        for way in range(4):
                            @pl.when(sends[way])
                            def _():
                                b_plane(g, s, 4 * m + k, way).wait_send()

                    b_sib(s, 4 * m + k).wait_send()

        return carry

    lax.fori_loop(0, NBC // 4, finish_b, 0)

    for n in range(NF):
        for way, (sends, device) in enumerate(f_ways):
            @pl.when(sends)
            def _():
                f_copy(n, way, device).wait_send()

    for which in range(2):
        @pl.when((p == 1) & (q == which))
        def _():
            m_copy(which).wait_send()

    a_store.wait()
    for g in range(2):
        @pl.when(c == g)
        def _():
            b_store(g).wait()

    f_store.wait()


def gather(kernel, noise):
    return pl.pallas_call(
        gather_kernel,
        out_shape=(
            jax.ShapeDtypeStruct((2, LOCAL, NB), F32),
            jax.ShapeDtypeStruct((2, NB, LOCAL), F32),
            jax.ShapeDtypeStruct((3 * NB, NB), F32),
        ),
        in_specs=[pl.BlockSpec(memory_space=pl.ANY), pl.BlockSpec(memory_space=pltpu.VMEM)],
        out_specs=[pl.BlockSpec(memory_space=pl.ANY)] * 3,
        scratch_shapes=[
            pltpu.VMEM((2, LOCAL, NB), F32),
            pltpu.VMEM((4, NB, LOCAL), F32),
            pltpu.VMEM((3 * NB, NB), F32),
            pltpu.VMEM((2, NB, NB), F32),
            pltpu.VMEM((NB, 2 * NB), F32),
            pltpu.SemaphoreType.DMA((2, NA)),
            pltpu.SemaphoreType.DMA((2, NA)),
            pltpu.SemaphoreType.DMA((2, NA)),
            pltpu.SemaphoreType.DMA((2, NA)),
            pltpu.SemaphoreType.DMA((4, NBC)),
            pltpu.SemaphoreType.DMA((5, 4, NBC)),
            pltpu.SemaphoreType.DMA((NF,)),
            pltpu.SemaphoreType.DMA((15, NF)),
            pltpu.SemaphoreType.DMA((2,)),
            pltpu.SemaphoreType.DMA((2,)),
            pltpu.SemaphoreType.DMA((3,)),
        ],
        compiler_params=pltpu.CompilerParams(
            collective_id=0, has_side_effects=True, vmem_limit_bytes=48 * 2**20
        ),
        name="gather_factor",
    )(kernel, noise)


def split(value):
    high = value.astype(jnp.bfloat16)
    return high, (value - high.astype(F32)).astype(jnp.bfloat16)


def three(a, b, dims):
    def one(u, v):
        return lax.dot_general(u, v, (dims, ((), ())), preferred_element_type=F32)

    return one(a[0], b[0]) + (one(a[0], b[1]) + one(a[1], b[0]))


NN = ((1,), (0,))
NT = ((1,), (1,))


def update_kernel(m_ref, noise_ref, a_ref, b_ref, f_ref, out_ref, cols_high, cols_low, f_high, f_low):
    p, q = lax.axis_index("row"), lax.axis_index("col")
    t = pl.program_id(0)

    @pl.when(t == 0)
    def _():
        f_high[...], f_low[...] = split(f_ref[...])

    x0, l10, x1 = [(f_high[k * NB : (k + 1) * NB, :], f_low[k * NB : (k + 1) * NB, :]) for k in range(3)]

    @pl.when(t == 0)
    def _():
        for col in range(T):
            at = slice(col * NB, (col + 1) * NB)
            col0 = split(three(x0, split(b_ref[0, :, at]), NN))
            col1 = split(three(x1, split(b_ref[1, :, at] - three(l10, col0, NN)), NN))
            for half, value in enumerate((col0, col1)):
                cols_high[half * NB : (half + 1) * NB, at] = value[0]
                cols_low[half * NB : (half + 1) * NB, at] = value[1]

    row0 = three(split(a_ref[0]), x0, NT)
    row0_parts = split(row0)
    row1 = three(split(a_ref[1] - three(row0_parts, l10, NT)), x1, NT)
    row1_parts = split(row1)
    rows = [jnp.concatenate([u, v], axis=1) for u, v in zip(row0_parts, row1_parts)]
    i = t * 16 + p
    i0 = lax.broadcasted_iota(jnp.int32, (NB, NB), 0)
    i1 = lax.broadcasted_iota(jnp.int32, (NB, NB), 1)
    for col in range(T):
        at = slice(col * NB, (col + 1) * NB)
        j = col * 16 + q
        panel = j < 2
        below = jnp.logical_not(panel) & (i >= j)

        @pl.when(below)
        def _():
            on_diag = (i0 == i1) & (i == j)
            block = m_ref[:, at] + jnp.where(on_diag, noise_ref[...], 0.0)
            out_ref[:, at] = block - three(rows, (cols_high[:, at], cols_low[:, at]), NN)

        @pl.when(panel & (i >= j))
        def _():
            value = jnp.where(q == 0, row0, row1)
            out_ref[:, at] = jnp.where((i == j) & (i0 < i1), 0.0, value)

        @pl.when(i < j)
        def _():
            out_ref[:, at] = m_ref[:, at]


def update(kernel, noise, a, b, f):
    return pl.pallas_call(
        update_kernel,
        grid=(T,),
        out_shape=jax.ShapeDtypeStruct((LOCAL, LOCAL), F32),
        in_specs=[
            pl.BlockSpec((NB, LOCAL), lambda t: (t, 0)),
            pl.BlockSpec((1, NB), lambda t: (0, t)),
            pl.BlockSpec((2, NB, NB), lambda t: (0, t, 0)),
            pl.BlockSpec((2, NB, LOCAL), lambda t: (0, 0, 0)),
            pl.BlockSpec((3 * NB, NB), lambda t: (0, 0)),
        ],
        out_specs=pl.BlockSpec((NB, LOCAL), lambda t: (t, 0)),
        scratch_shapes=[
            pltpu.VMEM((2 * NB, LOCAL), jnp.bfloat16),
            pltpu.VMEM((2 * NB, LOCAL), jnp.bfloat16),
            pltpu.VMEM((3 * NB, NB), jnp.bfloat16),
            pltpu.VMEM((3 * NB, NB), jnp.bfloat16),
        ],
        compiler_params=pltpu.CompilerParams(vmem_limit_bytes=48 * 2**20),
        name="update",
    )(kernel, noise, a, b, f)


def body(kernel, noise):
    noise = noise.reshape(1, LOCAL)
    a, b, f = gather(kernel, noise)
    return update(kernel, noise, a, b, f)


def solution(mesh):
    return jax.shard_map(
        body,
        mesh=mesh,
        in_specs=(P("row", "col"), P("row")),
        out_specs=P("row", "col"),
        check_vma=False,
    )
```

```python
import functools

import jax
import jax.numpy as jnp
from jax import lax
from jax.experimental import pallas as pl
from jax.experimental.pallas import tpu as pltpu
from jax.sharding import PartitionSpec as P

NB = 256
T = 5
LOCAL = NB * T
MESH = pl.DeviceIdType.MESH
HIGHEST = lax.Precision.HIGHEST
HIGH = lax.Precision.HIGH
F32 = jnp.float32

NA = 40
A_ROWS = LOCAL // NA
A_ONE = NA // 4
A_TURN = NA - A_ONE
HOP = 4
A_SLOTS = max(A_ONE + 7 * HOP, A_TURN + 4 * HOP)
NBC = 16
B_ROWS = NB // NBC
F_SLOT = 4
B_SLOTS = max(9, F_SLOT + 8)
PIECES = (
    ((0, 64, 128), (64, 64, 128), (128, 64, 256), (192, 64, 256))
    + tuple((NB + 64 * n, 64, 256) for n in range(4))
    + ((512, 64, 128), (576, 64, 128), (640, 64, 256), (704, 32, 256), (736, 32, 256))
)
STRIPS = 8
NF = len(PIECES)


def dot(a, b, dims, precision=HIGHEST):
    return lax.dot_general(a, b, (dims, ((), ())), precision=precision, preferred_element_type=F32)


def nn(a, b, precision=HIGHEST):
    return dot(a, b, ((1,), (0,)), precision)


def nt(a, b, precision=HIGHEST):
    return dot(a, b, ((1,), (1,)), precision)


def tn(a, b, precision=HIGHEST):
    return dot(a, b, ((0,), (0,)), precision)


def eliminate(rows, first):
    width = rows.shape[1]
    done = []
    for g in range(4):
        n = rows.shape[0]
        sub = lax.broadcasted_iota(jnp.int32, (n, 128), 0)
        at = first + 8 * g
        cols = [jnp.broadcast_to(rows[:, at + c : at + c + 1], (n, 128)) for c in range(8)]
        for j in range(8):
            inv = pltpu.reciprocal(cols[j][j : j + 1, :], approx=True)
            scale = jnp.where(sub > j, cols[j] * inv, 0.0)
            for c in range(j + 1, 8):
                cols[c] = cols[c] - scale * cols[c][j : j + 1, :]
            pivot = rows[j : j + 1, :]
            rows = jnp.concatenate(
                [rows[:, w : w + 128] - scale * pivot[:, w : w + 128] for w in range(0, width, 128)], axis=1
            )
        sub8 = lax.broadcasted_iota(jnp.int32, (8, 128), 0)
        diag = cols[0][:8]
        for j in range(1, 8):
            diag = jnp.where(sub8 == j, cols[j][:8], diag)
        root = lax.rsqrt(diag)
        done.append(rows[:8] * jnp.concatenate([root] * (width // 128), axis=1))
        rows = rows[8:]
    return jnp.concatenate(done, axis=0)


def factor_inverse(work, done=lambda k: None):
    following = None
    for k in range(8):
        r0 = 32 * k
        lo, hi = r0 // 128 * 128, NB + (r0 + 32 + 127) // 128 * 128
        rows = work[r0 : r0 + 32, lo:hi] if following is None else following
        rows = eliminate(rows, r0 - lo)
        work[r0 : r0 + 32, lo:hi] = rows
        done(k)
        if k == 7:
            break
        r1 = r0 + 32
        lo1, hi1 = r1 // 128 * 128, NB + (r1 + 32 + 127) // 128 * 128
        product = tn(rows[:, r1 - lo : r1 - lo + 32], rows)
        if hi1 > hi:
            product = jnp.concatenate([product, jnp.zeros((32, hi1 - hi), F32)], axis=1)
        following = work[r1 : r1 + 32, lo1:hi1] - product[:, lo1 - lo :]
        if k < 6:
            r2 = r1 + 32
            lo2 = r2 // 128 * 128
            product = tn(rows[:, lo2 - lo : NB - lo], rows[:, lo2 - lo :])
            work[r2:NB, lo2:hi] = work[r2:NB, lo2:hi] - product[r2 - lo2 :, :]


def identity():
    i0 = lax.broadcasted_iota(jnp.int32, (NB, NB), 0)
    i1 = lax.broadcasted_iota(jnp.int32, (NB, NB), 1)
    return i0 == i1


def gather_kernel(
    kernel_ref, noise_ref, a_out, b_out, f_out,
    a_buf, b_buf, f_buf, m_buf, work,
    a_recv, a_send, s_recv, s_send, b_recv, b_send, f_recv, f_send, m_recv, m_send, g_recv, g_send, local,
):
    p, q = lax.axis_index("row"), lax.axis_index("col")
    y, x, z, c = p // 4, p % 4, q // 2, q % 2
    rows_next = (y * 4 + (x + 1) % 4, (y + 1) % 4 * 4 + x, y * 4 + (x + 3) % 4, (y + 3) % 4 * 4 + x)
    z_next = ((z + 1) % 8, (z + 7) % 8)
    sib = (p, z * 2 + 1 - c)
    core0, core1 = c == 0, c == 1
    head = (p == 0) & (q == 0)
    a_source, b_source = z == 0, p < 2

    half = [pl.ds(k * NB, NB) for k in range(2)]
    side = [pl.ds(k * LOCAL, LOCAL) for k in range(2)]

    def a_load(s):
        return pltpu.make_async_copy(kernel_ref.at[:, pl.ds(0, NB)], a_buf.at[:, half[s]], local.at[0])

    def b_load(g, s):
        return pltpu.make_async_copy(kernel_ref.at[pl.ds(0, NB), :], b_buf.at[s, :, side[g]], local.at[1])

    def each_source(run_a, run_b):
        for s in range(2):
            @pl.when(a_source & (c == s))
            def _():
                run_a(s)

            for g in range(2):
                @pl.when((p == s) & (c == g))
                def _():
                    run_b(g, s)

    each_source(lambda s: a_load(s).start(), lambda g, s: b_load(g, s).start())
    for row in (0, 2 * NB):
        f_buf[row : row + 128, 128:] = jnp.zeros((128, 128), F32)

    barrier = pltpu.get_barrier_semaphore()
    peers = jnp.int32(7)

    def greet(device):
        pl.semaphore_signal(barrier, inc=1, device_id=device, device_id_type=MESH)

    for row in rows_next:
        greet((row, q))
    for level in z_next:
        greet((p, level * 2 + c))
    greet(sib)

    def greet_if(condition, devices):
        @pl.when(condition)
        def _():
            for device in devices:
                greet(device)

        return jnp.where(condition, len(devices), 0)

    peers += greet_if(head, [(0, 5), (0, 13), (1, 1)])
    peers += greet_if(((p == 0) & ((q == 5) | (q == 13))) | ((p == 1) & (q == 1)), [(0, 0)])
    peers += greet_if((p == 0) & (q == 5), [(0, 9)])
    peers += greet_if((p == 0) & (q == 9), [(0, 5)])
    peers += greet_if(core1 & (y == 0) & (x % 2 == 0), [((x + 2) % 4, q)])
    peers += greet_if(core1 & (y % 2 == 0), [((y + 2) % 4 * 4 + x, q)])

    each_source(lambda s: a_load(s).wait(), lambda g, s: b_load(g, s).wait())
    for s in range(2):
        @pl.when((p == s) & (q == s))
        def _():
            here = slice(s * NB, (s + 1) * NB)
            a_buf[:NB, here] = a_buf[:NB, here] + jnp.where(identity(), noise_ref[:, :NB], 0.0)

    pl.semaphore_wait(barrier, peers)

    def remote(src, dst, send_sem, recv_sem, device):
        return pltpu.make_async_remote_copy(
            src_ref=src, dst_ref=dst, send_sem=send_sem, recv_sem=recv_sem, device_id=device, device_id_type=MESH
        )

    def m_copy(which):
        return remote(a_buf.at[pl.ds(0, NB), half[which]], m_buf.at[which], m_send.at[which], m_recv.at[which], (0, 0))

    for which in range(2):
        @pl.when((p == 1) & (q == which))
        def _():
            m_copy(which).start()

    def a_ring(n, back):
        part = a_buf.at[pl.ds(n * A_ROWS, A_ROWS), :]
        return remote(part, part, a_send.at[back, n], a_recv.at[n], (p, z_next[back] * 2))

    def a_sib(n):
        part = a_buf.at[pl.ds(n * A_ROWS, A_ROWS), :]
        return remote(part, part, s_send.at[n], s_recv.at[n], sib)

    def a_join(s, i):
        part = a_buf.at[pl.ds(i * (LOCAL // 4), LOCAL // 4), half[s]]
        return remote(part, part, g_send.at[0, i], g_recv.at[0, i], sib)

    def b_plane(s, n, way):
        part = b_buf.at[s, pl.ds(n * B_ROWS, B_ROWS), :]
        return remote(part, part, b_send.at[way, s, n], b_recv.at[s, n], (rows_next[way], z * 2 + 1))

    def b_sib(s, n):
        part = b_buf.at[s, pl.ds(n * B_ROWS, B_ROWS), side[0]]
        return remote(part, part, b_send.at[4, s, n], b_recv.at[s, n], sib)

    def b_join(s, i):
        part = b_buf.at[s, pl.ds(i * (NB // 4), NB // 4), side[0]]
        return remote(part, part, g_send.at[1, i], g_recv.at[1, i], sib)

    a_hops = (z, 8 - z)

    def a_chunk(k, back):
        return jnp.where(k < A_ONE, 2 * k + back, A_ONE + k)

    def a_comes(k, back):
        return (k < A_ONE) | (a_hops[back] <= 4 - back)

    def a_more(k, back):
        return jnp.where(k < A_ONE, a_hops[back] < 7, a_hops[back] < 4 - back)

    def tree(s, k):
        dx, dy = (x + 4 - s) % 4, y
        u, v = ((dx, dy), (dy, (4 - dx) % 4), ((4 - dx) % 4, (4 - dy) % 4), ((4 - dy) % 4, dx))[k]
        hops = jnp.where(u == 0, 2, u) + jnp.minimum(v, 4 - v)
        sends = (
            (u == 2) | ((u == 1) & (v < 3)),
            (u == 1) & (v < 2),
            (u == 1) & (v >= 1),
            (v == 0) & ((u == 1) | (u == 2)),
        )
        return hops, [sends[(d - k) % 4] for d in range(4)]

    trees = {(s, k): tree(s, k) for s in range(2) for k in range(4)}

    def give_b(s):
        for i in range(4):
            b_join(s, i).start()

    each_source(
        lambda s: [a_join(s, i).start() for i in range(4)],
        lambda g, s: give_b(s) if g == 0 else None,
    )

    for s in range(2):
        @pl.when((p == s) & core1)
        def _():
            for i in range(4):
                b_join(s, i).wait_recv()
                for n in range(i * NBC // 4, (i + 1) * NBC // 4):
                    b_plane(s, n, n % 4).start()

    def a_first(k, carry):
        for back in range(2):
            a_ring(a_chunk(k, back), back).start()
        return carry

    @pl.when(a_source & core0)
    def _():
        a_join(1, 0).wait_recv()
        a_join(1, 1).wait_recv()
        lax.fori_loop(0, A_ONE, a_first, 0)
        a_join(1, 2).wait_recv()
        lax.fori_loop(A_ONE, 2 * A_ONE, a_first, 0)
        a_join(1, 3).wait_recv()
        lax.fori_loop(2 * A_ONE, A_TURN, a_first, 0)

    top = core1 & (p == 0)
    edge = core1 & (y == 0)
    every, large, strips = range(NF), range(STRIPS), range(STRIPS, NF)
    f_ways = [(head, (0, k), every) for k in (5, 13, 1)]
    f_ways += [(top & (z == 2), (0, 9), strips)] + [(top & (z == 2), (0, k), every) for k in (7, 3)] + [(top & (z == 6), (0, k), every) for k in (11, 15)]
    f_ways += [(top & (z == 5), (0, 9), large)]
    f_ways += [(top, (2, q), strips), (top, (1, q), every), (top, (3, q), every), (edge & (x == 1), (2, q), large)]
    f_ways += [(edge, (8 + x, q), strips), (edge, (4 + x, q), every), (edge, (12 + x, q), every)]
    f_ways += [(core1 & (y == 1), (8 + x, q), large)]
    f_ways += [(core1 & ((p != 0) | (q != 1)), sib, every)]
    F_HEAD = 3

    def f_copy(n, way, device):
        row, size, width = PIECES[n]
        part = f_buf.at[pl.ds(row, size), pl.ds(0, width)]
        return remote(part, part, f_send.at[way, n], f_recv.at[n], device)

    def pass_f(n):
        f_copy(n, 0, sib).wait_recv()
        for way in range(F_HEAD, len(f_ways)):
            if n in f_ways[way][2]:
                @pl.when(f_ways[way][0])
                def _():
                    f_copy(n, way, f_ways[way][1]).start()

    def far(v):
        return jnp.where(v == 0, 0, jnp.where(v == 2, 2, 1))

    f_slot = F_SLOT + far(x) + far(y) + jnp.where(z == 0, 0, jnp.where(z == 4, 3, jnp.where(z % 4 == 2, 1, 2)))

    def pass_a(slot, carry):
        @pl.when(core0 & (z != 0))
        def _():
            for back in range(2):
                m = slot - HOP * a_hops[back]
                k = (m + 3 * A_TURN) % A_TURN
                n = a_chunk(k, back)

                @pl.when((m >= 0) & (m < A_TURN) & a_comes(k, back))
                def _():
                    a_ring(n, back).wait_recv()

                    @pl.when(a_more(k, back))
                    def _():
                        a_ring(n, back).start()

                    a_sib(n).start()

        return carry

    def pass_b(slot, carry):
        @pl.when(core1)
        def _():
            for (s, k), (hops, sends) in trees.items():
                m = slot - hops
                n = 4 * ((m + NBC) % (NBC // 4)) + k

                @pl.when((p != s) & (m >= 0) & (m < NBC // 4))
                def _():
                    b_plane(s, n, 0).wait_recv()
                    for way in range(4):
                        @pl.when(sends[way])
                        def _():
                            b_plane(s, n, way).start()

                    b_sib(s, n).start()

            @pl.when(slot == f_slot)
            def _():
                for n in large:
                    pass_f(n)

        return carry

    lax.fori_loop(0, A_SLOTS, pass_a, 0)
    lax.fori_loop(0, B_SLOTS, pass_b, 0)

    def a_wait_sib():
        @pl.when(a_source)
        def _():
            for i in range(4):
                a_join(0, i).wait_recv()

        @pl.when(jnp.logical_not(a_source))
        def _():
            def wait(n, carry):
                a_sib(n).wait_recv()
                return carry

            lax.fori_loop(0, NA, wait, 0)

    def b_wait_sib(n, carry):
        for s in range(2):
            @pl.when(p != s)
            def _():
                b_sib(s, n).wait_recv()

        return carry

    a_store = pltpu.make_async_copy(a_buf, a_out, local.at[0])

    def b_store(g):
        return pltpu.make_async_copy(b_buf.at[:, :, side[g]], b_out, local.at[1])

    f_store = pltpu.make_async_copy(f_buf, f_out, local.at[2])

    @pl.when(head)
    def _():
        eye = jnp.where(identity(), 1.0, 0.0)

        def put(first, last, value):
            f_buf[first:last, :] = value
            for n in range(NF):
                if first <= PIECES[n][0] < last:
                    for way in range(F_HEAD):
                        f_copy(n, way, f_ways[way][1]).start()

        work[:, :NB] = a_buf[:NB, :NB]
        work[:, NB:] = eye
        factor_inverse(work)
        put(0, NB, work[:, NB:])
        m_copy(0).wait_recv()
        l10 = nt(m_buf[0], work[:, NB:])
        put(NB, 2 * NB, l10)
        m_copy(1).wait_recv()
        work[:, :NB] = m_buf[1] - nt(l10, l10)
        work[:, NB:] = eye

        def strip(k):
            last = 32 * (k + 1)
            for start, size, _ in PIECES:
                if start - 2 * NB + size == last:
                    put(start, start + size, work[last - size : last, NB:])

        factor_inverse(work, strip)
        lax.fori_loop(0, NBC, b_wait_sib, 0)
        a_store.start()
        b_store(0).start()

    @pl.when(core0 & jnp.logical_not(head))
    def _():
        a_store.start()
        lax.fori_loop(0, NBC, b_wait_sib, 0)
        b_store(0).start()
        for n in range(NF):
            f_copy(n, 0, sib).wait_recv()

    @pl.when(core1)
    def _():
        b_store(1).start()
        a_wait_sib()
        a_store.start()
        for n in strips:
            pass_f(n)

    f_store.start()

    each_source(
        lambda s: [a_join(s, i).wait_send() for i in range(4)],
        lambda g, s: [b_join(s, i).wait_send() for i in range(4)] if g == 0 else None,
    )

    def finish_a(k, carry):
        for back in range(2):
            n = a_chunk(k, back)

            @pl.when(core0 & (a_source | (a_comes(k, back) & a_more(k, back))))
            def _():
                a_ring(n, back).wait_send()

            @pl.when(core0 & (z != 0) & a_comes(k, back))
            def _():
                a_sib(n).wait_send()

        return carry

    lax.fori_loop(0, A_TURN, finish_a, 0)

    def finish_b(m, carry):
        @pl.when(core1)
        def _():
            for (s, k), (hops, sends) in trees.items():
                @pl.when(p == s)
                def _():
                    b_plane(s, 4 * m + k, k).wait_send()

                @pl.when(p != s)
                def _():
                    for way in range(4):
                        @pl.when(sends[way])
                        def _():
                            b_plane(s, 4 * m + k, way).wait_send()

                    b_sib(s, 4 * m + k).wait_send()

        return carry

    lax.fori_loop(0, NBC // 4, finish_b, 0)

    for n in range(NF):
        for way, (sends, device, pieces) in enumerate(f_ways):
            if n in pieces:
                @pl.when(sends)
                def _():
                    f_copy(n, way, device).wait_send()

    for which in range(2):
        @pl.when((p == 1) & (q == which))
        def _():
            m_copy(which).wait_send()

    a_store.wait()
    for g in range(2):
        @pl.when(c == g)
        def _():
            b_store(g).wait()

    f_store.wait()


def gather(kernel, noise):
    return pl.pallas_call(
        gather_kernel,
        out_shape=(
            jax.ShapeDtypeStruct((LOCAL, 2 * NB), F32),
            jax.ShapeDtypeStruct((2, NB, LOCAL), F32),
            jax.ShapeDtypeStruct((3 * NB, NB), F32),
        ),
        in_specs=[pl.BlockSpec(memory_space=pl.ANY), pl.BlockSpec(memory_space=pltpu.VMEM)],
        out_specs=[pl.BlockSpec(memory_space=pl.ANY)] * 3,
        scratch_shapes=[
            pltpu.VMEM((LOCAL, 2 * NB), F32),
            pltpu.VMEM((2, NB, 2 * LOCAL), F32),
            pltpu.VMEM((3 * NB, NB), F32),
            pltpu.VMEM((2, NB, NB), F32),
            pltpu.VMEM((NB, 2 * NB), F32),
            pltpu.SemaphoreType.DMA((NA,)),
            pltpu.SemaphoreType.DMA((2, NA)),
            pltpu.SemaphoreType.DMA((NA,)),
            pltpu.SemaphoreType.DMA((NA,)),
            pltpu.SemaphoreType.DMA((2, NBC)),
            pltpu.SemaphoreType.DMA((5, 2, NBC)),
            pltpu.SemaphoreType.DMA((NF,)),
            pltpu.SemaphoreType.DMA((18, NF)),
            pltpu.SemaphoreType.DMA((2,)),
            pltpu.SemaphoreType.DMA((2,)),
            pltpu.SemaphoreType.DMA((2, 4)),
            pltpu.SemaphoreType.DMA((2, 4)),
            pltpu.SemaphoreType.DMA((3,)),
        ],
        compiler_params=pltpu.CompilerParams(
            collective_id=0, has_side_effects=True, vmem_limit_bytes=48 * 2**20
        ),
        name="gather_factor",
    )(kernel, noise)


def split(value):
    high = value.astype(jnp.bfloat16)
    return high, (value - high.astype(F32)).astype(jnp.bfloat16)


def left(parts):
    return jnp.concatenate([parts[0], parts[0], parts[1]], axis=1)


def below(parts):
    return jnp.concatenate([parts[0], parts[1], parts[0]], axis=0)


def beside(parts):
    return jnp.concatenate([parts[0], parts[1], parts[0]], axis=1)


def product(a, b, dims=((1,), (0,))):
    return lax.dot_general(a, b, (dims, ((), ())), preferred_element_type=F32)


NT = ((1,), (1,))


def update_kernel(
    m_ref, noise_ref, a_ref, b_ref, f_ref, out_ref,
    m_buf, a_buf, b_buf, f_buf, rows, cols, m_sem, a_sem, b_sem, f_sem, out_sem,
):
    p, q = lax.axis_index("row"), lax.axis_index("col")
    strip = [pl.ds(t * NB, NB) for t in range(T)]
    f_load = pltpu.make_async_copy(f_ref, f_buf, f_sem)
    b_load = pltpu.make_async_copy(b_ref, b_buf, b_sem)
    a_load = pltpu.make_async_copy(a_ref, a_buf, a_sem)
    m_load = [pltpu.make_async_copy(m_ref.at[strip[t]], m_buf.at[strip[t]], m_sem.at[t]) for t in range(T)]
    store = [pltpu.make_async_copy(m_buf.at[strip[t]], out_ref.at[strip[t]], out_sem.at[t]) for t in range(T)]
    f_load.start()
    a_load.start()
    b_load.start()
    for t in range(T):
        m_load[t].start()

    f_load.wait()
    x0, l10, x1 = [split(f_buf[k * NB : (k + 1) * NB, :]) for k in range(3)]
    a_load.wait()
    row0 = product(left(split(a_buf[:, :NB])), beside(x0), NT)
    row0_parts = split(row0)
    row1 = product(left(split(a_buf[:, NB:] - product(left(row0_parts), beside(l10), NT))), beside(x1), NT)
    row1_parts = split(row1)
    for at, value in enumerate((row0_parts[0], row1_parts[0], row0_parts[1], row1_parts[1])):
        rows[:, at * NB : (at + 1) * NB] = value
    b_load.wait()
    col0 = split(product(left(x0), below(split(b_buf[0]))))
    col1 = split(product(left(x1), below(split(b_buf[1] - product(left(l10), below(col0))))))
    for at, value in enumerate((col0[0], col1[0], col0[1], col1[1])):
        cols[at * NB : (at + 1) * NB, :] = value

    for t in range(T):
        m_load[t].wait()
    i0 = lax.broadcasted_iota(jnp.int32, (NB, NB), 0)
    i1 = lax.broadcasted_iota(jnp.int32, (NB, NB), 1)
    for col in range(T):
        at = slice(col * NB, (col + 1) * NB)

        def blocks():
            high, low = slice(0, 2 * NB), slice(2 * NB, 4 * NB)
            u = jnp.concatenate([rows[col * NB :, high], rows[col * NB :, high], rows[col * NB :, low]], axis=1)
            v = jnp.concatenate([cols[high, at], cols[low, at], cols[high, at]], axis=0)
            value = m_buf[col * NB :, at] - product(u, v)
            first = value[:NB] + jnp.where((i0 == i1) & (p == q), noise_ref[:, at], 0.0)
            m_buf[at, at] = jnp.where(p >= q, first, m_buf[at, at])
            if col < T - 1:
                m_buf[(col + 1) * NB :, at] = value[NB:]

        if col > 0:
            blocks()
        else:
            pl.when(q >= 2)(blocks)

            @pl.when(q < 2)
            def _():
                panel = jnp.where(q == 0, row0, row1)
                first = jnp.where((p == q) & (i0 < i1), 0.0, panel[:NB])
                m_buf[at, at] = jnp.where(p >= q, first, m_buf[at, at])
                m_buf[NB:, at] = panel[NB:]

        store[col].start()
    for t in range(T):
        store[t].wait()


def update(kernel, noise, a, b, f):
    whole = pl.BlockSpec(memory_space=pl.ANY)
    return pl.pallas_call(
        update_kernel,
        out_shape=jax.ShapeDtypeStruct((LOCAL, LOCAL), F32),
        in_specs=[whole, pl.BlockSpec(memory_space=pltpu.VMEM), whole, whole, whole],
        out_specs=whole,
        scratch_shapes=[
            pltpu.VMEM((LOCAL, LOCAL), F32),
            pltpu.VMEM((LOCAL, 2 * NB), F32),
            pltpu.VMEM((2, NB, LOCAL), F32),
            pltpu.VMEM((3 * NB, NB), F32),
            pltpu.VMEM((LOCAL, 4 * NB), jnp.bfloat16),
            pltpu.VMEM((4 * NB, LOCAL), jnp.bfloat16),
            pltpu.SemaphoreType.DMA((T,)),
            pltpu.SemaphoreType.DMA,
            pltpu.SemaphoreType.DMA,
            pltpu.SemaphoreType.DMA,
            pltpu.SemaphoreType.DMA((T,)),
        ],
        compiler_params=pltpu.CompilerParams(vmem_limit_bytes=48 * 2**20),
        name="update",
    )(kernel, noise, a, b, f)


def body(kernel, noise):
    noise = noise.reshape(1, LOCAL)
    a, b, f = gather(kernel, noise)
    return update(kernel, noise, a, b, f)


def solution(mesh):
    return jax.shard_map(
        body,
        mesh=mesh,
        in_specs=(P("row", "col"), P("row")),
        out_specs=P("row", "col"),
        check_vma=False,
    )
```

```python
import functools

import jax
import jax.numpy as jnp
from jax import lax
from jax.experimental import pallas as pl
from jax.experimental.pallas import tpu as pltpu
from jax.sharding import PartitionSpec as P

NB = 256
T = 5
LOCAL = NB * T
MESH = pl.DeviceIdType.MESH
HIGHEST = lax.Precision.HIGHEST
HIGH = lax.Precision.HIGH
F32 = jnp.float32

NA = 40
A_ROWS = LOCAL // NA
A_ONE = NA // 4
A_TURN = NA - A_ONE
HOP = 4
A_SLOTS = max(A_ONE + 7 * HOP, A_TURN + 4 * HOP)
NBC = 16
B_ROWS = NB // NBC
F_SLOT = 4
B_SLOTS = max(9, F_SLOT + 8)
PIECES = (
    ((0, 64, 128), (64, 64, 128), (128, 64, 256), (192, 64, 256))
    + tuple((NB + 64 * n, 64, 256) for n in range(4))
    + ((512, 64, 128), (576, 64, 128), (640, 64, 256), (704, 32, 256), (736, 32, 256))
)
STRIPS = 8
NF = len(PIECES)


def dot(a, b, dims, precision=HIGHEST):
    return lax.dot_general(a, b, (dims, ((), ())), precision=precision, preferred_element_type=F32)


def nn(a, b, precision=HIGHEST):
    return dot(a, b, ((1,), (0,)), precision)


def nt(a, b, precision=HIGHEST):
    return dot(a, b, ((1,), (1,)), precision)


def tn(a, b, precision=HIGHEST):
    return dot(a, b, ((0,), (0,)), precision)


def eliminate(rows, first):
    width = rows.shape[1]
    done = []
    for g in range(4):
        n = rows.shape[0]
        sub = lax.broadcasted_iota(jnp.int32, (n, 128), 0)
        at = first + 8 * g
        cols = [jnp.broadcast_to(rows[:, at + c : at + c + 1], (n, 128)) for c in range(8)]
        for j in range(8):
            inv = pltpu.reciprocal(cols[j][j : j + 1, :], approx=True)
            scale = jnp.where(sub > j, cols[j] * inv, 0.0)
            for c in range(j + 1, 8):
                cols[c] = cols[c] - scale * cols[c][j : j + 1, :]
            pivot = rows[j : j + 1, :]
            rows = jnp.concatenate(
                [rows[:, w : w + 128] - scale * pivot[:, w : w + 128] for w in range(0, width, 128)], axis=1
            )
        sub8 = lax.broadcasted_iota(jnp.int32, (8, 128), 0)
        diag = cols[0][:8]
        for j in range(1, 8):
            diag = jnp.where(sub8 == j, cols[j][:8], diag)
        root = lax.rsqrt(diag)
        done.append(rows[:8] * jnp.concatenate([root] * (width // 128), axis=1))
        rows = rows[8:]
    return jnp.concatenate(done, axis=0)


def factor_inverse(work, done=lambda k: None):
    following = None
    for k in range(8):
        r0 = 32 * k
        lo, hi = r0 // 128 * 128, NB + (r0 + 32 + 127) // 128 * 128
        rows = work[r0 : r0 + 32, lo:hi] if following is None else following
        rows = eliminate(rows, r0 - lo)
        work[r0 : r0 + 32, lo:hi] = rows
        done(k)
        if k == 7:
            break
        r1 = r0 + 32
        lo1, hi1 = r1 // 128 * 128, NB + (r1 + 32 + 127) // 128 * 128
        product = tn(rows[:, r1 - lo : r1 - lo + 32], rows)
        if hi1 > hi:
            product = jnp.concatenate([product, jnp.zeros((32, hi1 - hi), F32)], axis=1)
        following = work[r1 : r1 + 32, lo1:hi1] - product[:, lo1 - lo :]
        if k < 6:
            r2 = r1 + 32
            lo2 = r2 // 128 * 128
            product = tn(rows[:, lo2 - lo : NB - lo], rows[:, lo2 - lo :])
            work[r2:NB, lo2:hi] = work[r2:NB, lo2:hi] - product[r2 - lo2 :, :]


def identity():
    i0 = lax.broadcasted_iota(jnp.int32, (NB, NB), 0)
    i1 = lax.broadcasted_iota(jnp.int32, (NB, NB), 1)
    return i0 == i1


def gather_kernel(
    kernel_ref, noise_ref, a_out, b_out, f_out,
    a_buf, b_buf, f_buf, m_buf, work,
    a_recv, a_send, s_recv, s_send, b_recv, b_send, f_recv, f_send, m_recv, m_send, g_recv, g_send, t_recv, t_send, h_recv, local,
):
    p, q = lax.axis_index("row"), lax.axis_index("col")
    y, x, z, c = p // 4, p % 4, q // 2, q % 2
    rows_next = (y * 4 + (x + 1) % 4, (y + 1) % 4 * 4 + x, y * 4 + (x + 3) % 4, (y + 3) % 4 * 4 + x)
    z_next = ((z + 1) % 8, (z + 7) % 8)
    sib = (p, z * 2 + 1 - c)
    core0, core1 = c == 0, c == 1
    head = (p == 0) & (q == 0)
    a_source, b_source = z == 0, p < 2

    half = [pl.ds(k * NB, NB) for k in range(2)]
    side = [pl.ds(k * LOCAL, LOCAL) for k in range(2)]

    def a_load(s):
        return pltpu.make_async_copy(kernel_ref.at[:, pl.ds(0, NB)], a_buf.at[:, half[s]], local.at[0])

    def b_load(g, s):
        return pltpu.make_async_copy(kernel_ref.at[pl.ds(0, NB), :], b_buf.at[s, :, side[g]], local.at[1])

    def each_source(run_a, run_b):
        for s in range(2):
            @pl.when(a_source & (c == s))
            def _():
                run_a(s)

            for g in range(2):
                @pl.when((p == s) & (c == g))
                def _():
                    run_b(g, s)

    each_source(lambda s: a_load(s).start(), lambda g, s: b_load(g, s).start())
    for row in (0, 2 * NB):
        f_buf[row : row + 128, 128:] = jnp.zeros((128, 128), F32)

    barrier = pltpu.get_barrier_semaphore()
    peers = jnp.int32(7)

    def greet(device):
        pl.semaphore_signal(barrier, inc=1, device_id=device, device_id_type=MESH)

    for row in rows_next:
        greet((row, q))
    for level in z_next:
        greet((p, level * 2 + c))
    greet(sib)

    def greet_if(condition, devices):
        @pl.when(condition)
        def _():
            for device in devices:
                greet(device)

        return jnp.where(condition, len(devices), 0)

    peers += greet_if(head, [(0, 5), (0, 13), (1, 1)])
    peers += greet_if(((p == 0) & ((q == 5) | (q == 13))) | ((p == 1) & (q == 1)), [(0, 0)])
    peers += greet_if((p == 0) & (q == 5), [(0, 9)])
    peers += greet_if((p == 0) & (q == 9), [(0, 5)])
    peers += greet_if(core1 & (y == 0) & (x % 2 == 0), [((x + 2) % 4, q)])
    peers += greet_if(core1 & (y % 2 == 0), [((y + 2) % 4 * 4 + x, q)])

    each_source(lambda s: a_load(s).wait(), lambda g, s: b_load(g, s).wait())
    for s in range(2):
        @pl.when((p == s) & (q == s))
        def _():
            here = slice(s * NB, (s + 1) * NB)
            a_buf[:NB, here] = a_buf[:NB, here] + jnp.where(identity(), noise_ref[:, :NB], 0.0)

    pl.semaphore_wait(barrier, peers)

    def remote(src, dst, send_sem, recv_sem, device):
        return pltpu.make_async_remote_copy(
            src_ref=src, dst_ref=dst, send_sem=send_sem, recv_sem=recv_sem, device_id=device, device_id_type=MESH
        )

    def m_copy(which):
        return remote(a_buf.at[pl.ds(0, NB), half[which]], m_buf.at[which], m_send.at[which], m_recv.at[which], (0, 0))

    for which in range(2):
        @pl.when((p == 1) & (q == which))
        def _():
            m_copy(which).start()

    def a_ring(n, back):
        part = a_buf.at[pl.ds(n * A_ROWS, A_ROWS), :]
        return remote(part, part, a_send.at[back, jnp.where(n < 2 * A_ONE, 0, 1)], a_recv.at[n], (p, z_next[back] * 2))

    def a_sib(first, count):
        part = a_buf.at[pl.ds(first * A_ROWS, count * A_ROWS), :]
        return remote(part, part, s_send, s_recv, sib)

    def a_sent(back, group):
        part = a_buf.at[pl.ds(0, (A_ONE, A_TURN - A_ONE)[group] * A_ROWS), :]
        return remote(part, part, a_send.at[back, group], a_recv.at[0], (p, z_next[back] * 2))

    def a_join(s, i):
        part = a_buf.at[pl.ds(i * (LOCAL // 4), LOCAL // 4), half[s]]
        return remote(part, part, g_send.at[0, i], g_recv.at[0, i], sib)

    def b_plane(s, n, k, way):
        part = b_buf.at[s, pl.ds(n * B_ROWS, B_ROWS), :]
        return remote(part, part, b_send.at[way, s, k], b_recv.at[s, n], (rows_next[way], z * 2 + 1))

    def b_sent(s, k, way):
        part = b_buf.at[s, pl.ds(0, NB // 4), :]
        return remote(part, part, b_send.at[way, s, k], b_recv.at[s, 0], (rows_next[way], z * 2 + 1))

    def b_sib(s, first, count):
        part = b_buf.at[s, pl.ds(first * (NB // 4), count * (NB // 4)), side[0]]
        return remote(part, part, t_send.at[s], t_recv.at[s], sib)

    def b_join(s, i):
        part = b_buf.at[s, pl.ds(i * (NB // 4), NB // 4), side[0]]
        return remote(part, part, g_send.at[1, i], g_recv.at[1, i], sib)

    a_hops = (z, 8 - z)

    def a_chunk(k, back):
        return jnp.where(k < A_ONE, 2 * k + back, A_ONE + k)

    def a_comes(k, back):
        return (k < A_ONE) | (a_hops[back] <= 4 - back)

    def a_more(k, back):
        return jnp.where(k < A_ONE, a_hops[back] < 7, a_hops[back] < 4 - back)

    def tree(s, k):
        dx, dy = (x + 4 - s) % 4, y
        u, v = ((dx, dy), (dy, (4 - dx) % 4), ((4 - dx) % 4, (4 - dy) % 4), ((4 - dy) % 4, dx))[k]
        hops = jnp.where(u == 0, 2, u) + jnp.minimum(v, 4 - v)
        sends = (
            (u == 2) | ((u == 1) & (v < 3)),
            (u == 1) & (v < 2),
            (u == 1) & (v >= 1),
            (v == 0) & ((u == 1) | (u == 2)),
        )
        return hops, [sends[(d - k) % 4] for d in range(4)]

    trees = {(s, k): tree(s, k) for s in range(2) for k in range(4)}
    b_last = []
    for s in range(2):
        last = trees[s, 0][0]
        for k in range(1, 4):
            last = jnp.where(trees[s, k][0] > last, trees[s, k][0], last)
        b_last.append(last)


    def give_b(s):
        for i in range(4):
            b_join(s, i).start()

    each_source(
        lambda s: [a_join(s, i).start() for i in range(4)],
        lambda g, s: give_b(s) if g == 0 else None,
    )

    for s in range(2):
        @pl.when((p == s) & core1)
        def _():
            for i in range(4):
                b_join(s, i).wait_recv()
                for n in range(i * NBC // 4, (i + 1) * NBC // 4):
                    b_plane(s, n, n % 4, n % 4).start()

    def a_first(k, carry):
        for back in range(2):
            a_ring(a_chunk(k, back), back).start()
        return carry

    @pl.when(a_source & core0)
    def _():
        a_join(1, 0).wait_recv()
        a_join(1, 1).wait_recv()
        lax.fori_loop(0, A_ONE, a_first, 0)
        a_join(1, 2).wait_recv()
        lax.fori_loop(A_ONE, 2 * A_ONE, a_first, 0)
        a_join(1, 3).wait_recv()
        lax.fori_loop(2 * A_ONE, A_TURN, a_first, 0)

    top = core1 & (p == 0)
    edge = core1 & (y == 0)
    every, large, strips = range(NF), range(STRIPS), range(STRIPS, NF)
    f_ways = [(head, (0, k), every) for k in (5, 13, 1)]
    f_ways += [(top & (z == 2), (0, 9), strips)] + [(top & (z == 2), (0, k), every) for k in (7, 3)] + [(top & (z == 6), (0, k), every) for k in (11, 15)]
    f_ways += [(top & (z == 5), (0, 9), large)]
    f_ways += [(top, (2, q), strips), (top, (1, q), every), (top, (3, q), every), (edge & (x == 1), (2, q), large)]
    f_ways += [(edge, (8 + x, q), strips), (edge, (4 + x, q), every), (edge, (12 + x, q), every)]
    f_ways += [(core1 & (y == 1), (8 + x, q), large)]
    f_ways += [(core1 & ((p != 0) | (q != 1)), sib, every)]
    F_HEAD = 3

    def f_copy(n, way, device):
        row, size, width = PIECES[n]
        part = f_buf.at[pl.ds(row, size), pl.ds(0, width)]
        if way == len(f_ways) - 1:
            return remote(part, part, f_send.at[way], h_recv, device)
        return remote(part, part, f_send.at[way], f_recv.at[n], device)

    def f_whole(way, pieces):
        part = f_buf.at[pl.ds(0, sum(PIECES[n][1] * PIECES[n][2] for n in pieces) // NB), :]
        return remote(part, part, f_send.at[way], h_recv, sib)


    def pass_f(n):
        f_copy(n, 0, sib).wait_recv()
        for way in range(F_HEAD, len(f_ways)):
            if n in f_ways[way][2]:
                @pl.when(f_ways[way][0])
                def _():
                    f_copy(n, way, f_ways[way][1]).start()

    def far(v):
        return jnp.where(v == 0, 0, jnp.where(v == 2, 2, 1))

    f_slot = F_SLOT + far(x) + far(y) + jnp.where(z == 0, 0, jnp.where(z == 4, 3, jnp.where(z % 4 == 2, 1, 2)))

    def pass_a(slot, carry):
        @pl.when(core0 & (z != 0))
        def _():
            for back in range(2):
                m = slot - HOP * a_hops[back]
                k = (m + 3 * A_TURN) % A_TURN
                n = a_chunk(k, back)

                @pl.when((m >= 0) & (m < A_TURN) & a_comes(k, back))
                def _():
                    a_ring(n, back).wait_recv()

                    @pl.when(a_more(k, back))
                    def _():
                        a_ring(n, back).start()

                    a_sib(n, 1).start()

        return carry

    def pass_b(slot, carry):
        @pl.when(core1)
        def _():
            for (s, k), (hops, sends) in trees.items():
                m = slot - hops
                n = 4 * ((m + NBC) % (NBC // 4)) + k

                @pl.when((p != s) & (m >= 0) & (m < NBC // 4))
                def _():
                    b_plane(s, n, k, 0).wait_recv()
                    for way in range(4):
                        @pl.when(sends[way])
                        def _():
                            b_plane(s, n, k, way).start()

            for s in range(2):
                m = slot - b_last[s]

                @pl.when((p != s) & (m >= 0) & (m < 4))
                def _():
                    b_sib(s, (m + NBC) % 4, 1).start()

            @pl.when(slot == f_slot)
            def _():
                for n in large:
                    pass_f(n)

        return carry

    lax.fori_loop(0, A_SLOTS, pass_a, 0)
    lax.fori_loop(0, B_SLOTS, pass_b, 0)

    def a_wait_sib():
        @pl.when(a_source)
        def _():
            for i in range(4):
                a_join(0, i).wait_recv()

        @pl.when(jnp.logical_not(a_source))
        def _():
            a_sib(0, NA).wait_recv()

    def b_wait_sib():
        for s in range(2):
            @pl.when(p != s)
            def _():
                b_sib(s, 0, 4).wait_recv()

    a_store = pltpu.make_async_copy(a_buf, a_out, local.at[0])

    def b_store(g):
        return pltpu.make_async_copy(b_buf.at[:, :, side[g]], b_out, local.at[1])

    f_store = pltpu.make_async_copy(f_buf, f_out, local.at[2])

    @pl.when(head)
    def _():
        eye = jnp.where(identity(), 1.0, 0.0)

        def put(first, last, value):
            f_buf[first:last, :] = value
            for n in range(NF):
                if first <= PIECES[n][0] < last:
                    for way in range(F_HEAD):
                        f_copy(n, way, f_ways[way][1]).start()

        work[:, :NB] = a_buf[:NB, :NB]
        work[:, NB:] = eye
        factor_inverse(work)
        put(0, NB, work[:, NB:])
        m_copy(0).wait_recv()
        l10 = nt(m_buf[0], work[:, NB:])
        put(NB, 2 * NB, l10)
        m_copy(1).wait_recv()
        work[:, :NB] = m_buf[1] - nt(l10, l10)
        work[:, NB:] = eye

        def strip(k):
            last = 32 * (k + 1)
            for start, size, _ in PIECES:
                if start - 2 * NB + size == last:
                    put(start, start + size, work[last - size : last, NB:])

        factor_inverse(work, strip)
        b_wait_sib()
        a_store.start()
        b_store(0).start()

    @pl.when(core0 & jnp.logical_not(head))
    def _():
        a_store.start()
        b_wait_sib()
        b_store(0).start()
        f_whole(0, every).wait_recv()

    @pl.when(core1)
    def _():
        b_store(1).start()
        for n in strips:
            pass_f(n)

        a_wait_sib()
        a_store.start()

    f_store.start()

    each_source(
        lambda s: [a_join(s, i).wait_send() for i in range(4)],
        lambda g, s: [b_join(s, i).wait_send() for i in range(4)] if g == 0 else None,
    )

    for back in range(2):
        for group, k in enumerate((0, A_ONE)):
            @pl.when(core0 & (a_source | (a_comes(k, back) & a_more(k, back))))
            def _():
                a_sent(back, group).wait_send()

    @pl.when(core0 & (z != 0))
    def _():
        a_sib(0, NA).wait_send()

    for (s, k), (hops, sends) in trees.items():
        for way in range(4):
            mine = jnp.where(p == s, way == k, sends[way])

            @pl.when(core1 & mine)
            def _():
                b_sent(s, k, way).wait_send()

    for s in range(2):
        @pl.when(core1 & (p != s))
        def _():
            b_sib(s, 0, 4).wait_send()

    for way, (sends, device, pieces) in enumerate(f_ways):
        @pl.when(sends)
        def _():
            f_whole(way, pieces).wait_send()

    for which in range(2):
        @pl.when((p == 1) & (q == which))
        def _():
            m_copy(which).wait_send()

    a_store.wait()
    for g in range(2):
        @pl.when(c == g)
        def _():
            b_store(g).wait()

    f_store.wait()


def gather(kernel, noise):
    return pl.pallas_call(
        gather_kernel,
        out_shape=(
            jax.ShapeDtypeStruct((LOCAL, 2 * NB), F32),
            jax.ShapeDtypeStruct((2, NB, LOCAL), F32),
            jax.ShapeDtypeStruct((3 * NB, NB), F32),
        ),
        in_specs=[pl.BlockSpec(memory_space=pl.ANY), pl.BlockSpec(memory_space=pltpu.VMEM)],
        out_specs=[pl.BlockSpec(memory_space=pl.ANY)] * 3,
        scratch_shapes=[
            pltpu.VMEM((LOCAL, 2 * NB), F32),
            pltpu.VMEM((2, NB, 2 * LOCAL), F32),
            pltpu.VMEM((3 * NB, NB), F32),
            pltpu.VMEM((2, NB, NB), F32),
            pltpu.VMEM((NB, 2 * NB), F32),
            pltpu.SemaphoreType.DMA((NA,)),
            pltpu.SemaphoreType.DMA((2, 2)),
            pltpu.SemaphoreType.DMA,
            pltpu.SemaphoreType.DMA,
            pltpu.SemaphoreType.DMA((2, NBC)),
            pltpu.SemaphoreType.DMA((4, 2, 4)),
            pltpu.SemaphoreType.DMA((NF,)),
            pltpu.SemaphoreType.DMA((18,)),
            pltpu.SemaphoreType.DMA((2,)),
            pltpu.SemaphoreType.DMA((2,)),
            pltpu.SemaphoreType.DMA((2, 4)),
            pltpu.SemaphoreType.DMA((2, 4)),
            pltpu.SemaphoreType.DMA((2,)),
            pltpu.SemaphoreType.DMA((2,)),
            pltpu.SemaphoreType.DMA,
            pltpu.SemaphoreType.DMA((3,)),
        ],
        compiler_params=pltpu.CompilerParams(
            collective_id=0, has_side_effects=True, vmem_limit_bytes=48 * 2**20
        ),
        name="gather_factor",
    )(kernel, noise)


def split(value):
    high = value.astype(jnp.bfloat16)
    return high, (value - high.astype(F32)).astype(jnp.bfloat16)


def left(parts):
    return jnp.concatenate([parts[0], parts[0], parts[1]], axis=1)


def below(parts):
    return jnp.concatenate([parts[0], parts[1], parts[0]], axis=0)


def beside(parts):
    return jnp.concatenate([parts[0], parts[1], parts[0]], axis=1)


def product(a, b, dims=((1,), (0,))):
    return lax.dot_general(a, b, (dims, ((), ())), preferred_element_type=F32)


NT = ((1,), (1,))


def update_kernel(
    m_ref, noise_ref, a_ref, b_ref, f_ref, out_ref,
    m_buf, a_buf, b_buf, f_buf, rows, cols, m_sem, a_sem, b_sem, f_sem, out_sem,
):
    p, q = lax.axis_index("row"), lax.axis_index("col")
    strip = [pl.ds(t * NB, NB) for t in range(T)]
    f_load = pltpu.make_async_copy(f_ref, f_buf, f_sem)
    b_load = pltpu.make_async_copy(b_ref, b_buf, b_sem)
    a_load = pltpu.make_async_copy(a_ref, a_buf, a_sem)
    m_load = [pltpu.make_async_copy(m_ref.at[strip[t]], m_buf.at[strip[t]], m_sem.at[t]) for t in range(T)]
    store = [pltpu.make_async_copy(m_buf.at[strip[t]], out_ref.at[strip[t]], out_sem.at[t]) for t in range(T)]
    f_load.start()
    a_load.start()
    b_load.start()
    for t in range(T):
        m_load[t].start()

    f_load.wait()
    x0, l10, x1 = [split(f_buf[k * NB : (k + 1) * NB, :]) for k in range(3)]
    a_load.wait()
    row0 = product(left(split(a_buf[:, :NB])), beside(x0), NT)
    row0_parts = split(row0)
    row1 = product(left(split(a_buf[:, NB:] - product(left(row0_parts), beside(l10), NT))), beside(x1), NT)
    row1_parts = split(row1)
    for at, value in enumerate((row0_parts[0], row1_parts[0], row0_parts[1], row1_parts[1])):
        rows[:, at * NB : (at + 1) * NB] = value
    b_load.wait()
    col0 = split(product(left(x0), below(split(b_buf[0]))))
    col1 = split(product(left(x1), below(split(b_buf[1] - product(left(l10), below(col0))))))
    for at, value in enumerate((col0[0], col1[0], col0[1], col1[1])):
        cols[at * NB : (at + 1) * NB, :] = value

    for t in range(T):
        m_load[t].wait()
    i0 = lax.broadcasted_iota(jnp.int32, (NB, NB), 0)
    i1 = lax.broadcasted_iota(jnp.int32, (NB, NB), 1)
    for col in range(T):
        at = slice(col * NB, (col + 1) * NB)

        def blocks():
            high, low = slice(0, 2 * NB), slice(2 * NB, 4 * NB)
            u = jnp.concatenate([rows[col * NB :, high], rows[col * NB :, high], rows[col * NB :, low]], axis=1)
            v = jnp.concatenate([cols[high, at], cols[low, at], cols[high, at]], axis=0)
            value = m_buf[col * NB :, at] - product(u, v)
            first = value[:NB] + jnp.where((i0 == i1) & (p == q), noise_ref[:, at], 0.0)
            m_buf[at, at] = jnp.where(p >= q, first, m_buf[at, at])
            if col < T - 1:
                m_buf[(col + 1) * NB :, at] = value[NB:]

        if col > 0:
            blocks()
        else:
            pl.when(q >= 2)(blocks)

            @pl.when(q < 2)
            def _():
                panel = jnp.where(q == 0, row0, row1)
                first = jnp.where((p == q) & (i0 < i1), 0.0, panel[:NB])
                m_buf[at, at] = jnp.where(p >= q, first, m_buf[at, at])
                m_buf[NB:, at] = panel[NB:]

        store[col].start()
    for t in range(T):
        store[t].wait()


def update(kernel, noise, a, b, f):
    whole = pl.BlockSpec(memory_space=pl.ANY)
    return pl.pallas_call(
        update_kernel,
        out_shape=jax.ShapeDtypeStruct((LOCAL, LOCAL), F32),
        in_specs=[whole, pl.BlockSpec(memory_space=pltpu.VMEM), whole, whole, whole],
        out_specs=whole,
        scratch_shapes=[
            pltpu.VMEM((LOCAL, LOCAL), F32),
            pltpu.VMEM((LOCAL, 2 * NB), F32),
            pltpu.VMEM((2, NB, LOCAL), F32),
            pltpu.VMEM((3 * NB, NB), F32),
            pltpu.VMEM((LOCAL, 4 * NB), jnp.bfloat16),
            pltpu.VMEM((4 * NB, LOCAL), jnp.bfloat16),
            pltpu.SemaphoreType.DMA((T,)),
            pltpu.SemaphoreType.DMA,
            pltpu.SemaphoreType.DMA,
            pltpu.SemaphoreType.DMA,
            pltpu.SemaphoreType.DMA((T,)),
        ],
        compiler_params=pltpu.CompilerParams(vmem_limit_bytes=48 * 2**20),
        name="update",
    )(kernel, noise, a, b, f)


def body(kernel, noise):
    noise = noise.reshape(1, LOCAL)
    a, b, f = gather(kernel, noise)
    return update(kernel, noise, a, b, f)


def solution(mesh):
    return jax.shard_map(
        body,
        mesh=mesh,
        in_specs=(P("row", "col"), P("row")),
        out_specs=P("row", "col"),
        check_vma=False,
    )
```

```python
import functools

import jax
import jax.numpy as jnp
from jax import lax
from jax.experimental import pallas as pl
from jax.experimental.pallas import tpu as pltpu
from jax.sharding import PartitionSpec as P

NB = 256
T = 5
LOCAL = NB * T
MESH = pl.DeviceIdType.MESH
HIGHEST = lax.Precision.HIGHEST
HIGH = lax.Precision.HIGH
F32 = jnp.float32

NA = 20
A_ROWS = LOCAL // NA
A_ONE = NA // 4
A_TURN = NA - A_ONE
HOP = 3
A_SLOTS = max(A_ONE + 7 * HOP, A_TURN + 4 * HOP)
NBC = 16
B_ROWS = NB // NBC
F_SLOT = 3
B_SLOTS = max(9, F_SLOT + 8)
PIECES = (
    ((0, 64, 128), (64, 64, 128), (128, 64, 256), (192, 64, 256))
    + tuple((NB + 64 * n, 64, 256) for n in range(4))
    + ((512, 64, 128), (576, 64, 128), (640, 64, 256), (704, 32, 256), (736, 32, 256))
)
STRIPS = 8
NF = len(PIECES)


def dot(a, b, dims, precision=HIGHEST):
    return lax.dot_general(a, b, (dims, ((), ())), precision=precision, preferred_element_type=F32)


def nn(a, b, precision=HIGHEST):
    return dot(a, b, ((1,), (0,)), precision)


def nt(a, b, precision=HIGHEST):
    return dot(a, b, ((1,), (1,)), precision)


def tn(a, b, precision=HIGHEST):
    return dot(a, b, ((0,), (0,)), precision)


def eliminate(rows, first):
    width = rows.shape[1]
    done = []
    for g in range(4):
        n = rows.shape[0]
        sub = lax.broadcasted_iota(jnp.int32, (n, 128), 0)
        at = first + 8 * g
        cols = [jnp.broadcast_to(rows[:, at + c : at + c + 1], (n, 128)) for c in range(8)]
        for j in range(8):
            inv = pltpu.reciprocal(cols[j][j : j + 1, :], approx=True)
            scale = jnp.where(sub > j, cols[j] * inv, 0.0)
            for c in range(j + 1, 8):
                cols[c] = cols[c] - scale * cols[c][j : j + 1, :]
            pivot = rows[j : j + 1, :]
            rows = jnp.concatenate(
                [rows[:, w : w + 128] - scale * pivot[:, w : w + 128] for w in range(0, width, 128)], axis=1
            )
        sub8 = lax.broadcasted_iota(jnp.int32, (8, 128), 0)
        diag = cols[0][:8]
        for j in range(1, 8):
            diag = jnp.where(sub8 == j, cols[j][:8], diag)
        root = lax.rsqrt(diag)
        done.append(rows[:8] * jnp.concatenate([root] * (width // 128), axis=1))
        rows = rows[8:]
    return jnp.concatenate(done, axis=0)


def factor_inverse(work, done=lambda k: None):
    following = None
    for k in range(8):
        r0 = 32 * k
        lo, hi = r0 // 128 * 128, NB + (r0 + 32 + 127) // 128 * 128
        rows = work[r0 : r0 + 32, lo:hi] if following is None else following
        rows = eliminate(rows, r0 - lo)
        work[r0 : r0 + 32, lo:hi] = rows
        done(k)
        if k == 7:
            break
        r1 = r0 + 32
        lo1, hi1 = r1 // 128 * 128, NB + (r1 + 32 + 127) // 128 * 128
        product = tn(rows[:, r1 - lo : r1 - lo + 32], rows)
        if hi1 > hi:
            product = jnp.concatenate([product, jnp.zeros((32, hi1 - hi), F32)], axis=1)
        following = work[r1 : r1 + 32, lo1:hi1] - product[:, lo1 - lo :]
        if k < 6:
            r2 = r1 + 32
            lo2 = r2 // 128 * 128
            product = tn(rows[:, lo2 - lo : NB - lo], rows[:, lo2 - lo :])
            work[r2:NB, lo2:hi] = work[r2:NB, lo2:hi] - product[r2 - lo2 :, :]


def identity():
    i0 = lax.broadcasted_iota(jnp.int32, (NB, NB), 0)
    i1 = lax.broadcasted_iota(jnp.int32, (NB, NB), 1)
    return i0 == i1


def gather_kernel(
    kernel_ref, noise_ref, a_out, b_out, f_out,
    a_buf, b_buf, f_buf, m_buf, work,
    a_recv, a_send, s_recv, s_send, b_recv, b_send, f_recv, f_send, m_recv, m_send, g_recv, g_send, o_recv, r_recv, t_recv, t_send, h_recv, local,
):
    p, q = lax.axis_index("row"), lax.axis_index("col")
    y, x, z, c = p // 4, p % 4, q // 2, q % 2
    rows_next = (y * 4 + (x + 1) % 4, (y + 1) % 4 * 4 + x, y * 4 + (x + 3) % 4, (y + 3) % 4 * 4 + x)
    z_next = ((z + 1) % 8, (z + 7) % 8)
    sib = (p, z * 2 + 1 - c)
    core0, core1 = c == 0, c == 1
    head = (p == 0) & (q == 0)
    a_source, b_source = z == 0, p < 2

    half = [pl.ds(k * NB, NB) for k in range(2)]
    side = [pl.ds(k * LOCAL, LOCAL) for k in range(2)]

    def a_load(s):
        return pltpu.make_async_copy(kernel_ref.at[:, pl.ds(0, NB)], a_buf.at[:, half[s]], local.at[0])

    def b_load(g, s):
        return pltpu.make_async_copy(kernel_ref.at[pl.ds(0, NB), :], b_buf.at[s, :, side[g]], local.at[1])

    def each_source(run_a, run_b):
        for s in range(2):
            @pl.when(a_source & (c == s))
            def _():
                run_a(s)

            for g in range(2):
                @pl.when((p == s) & (c == g))
                def _():
                    run_b(g, s)

    each_source(lambda s: a_load(s).start(), lambda g, s: b_load(g, s).start())
    for row in (0, 2 * NB):
        f_buf[row : row + 128, 128:] = jnp.zeros((128, 128), F32)

    barrier = pltpu.get_barrier_semaphore()
    peers = jnp.int32(7)

    def greet(device):
        pl.semaphore_signal(barrier, inc=1, device_id=device, device_id_type=MESH)

    for row in rows_next:
        greet((row, q))
    for level in z_next:
        greet((p, level * 2 + c))
    greet(sib)

    def greet_if(condition, devices):
        @pl.when(condition)
        def _():
            for device in devices:
                greet(device)

        return jnp.where(condition, len(devices), 0)

    peers += greet_if(a_source & core1, [(p, 2), (p, 14)])
    peers += greet_if(core0 & ((z == 1) | (z == 7)), [(p, 1)])
    peers += greet_if(b_source & core0, [(row, z * 2 + 1) for row in rows_next])
    for s in range(2):
        near = ((y == 0) & ((x + 4 - s) % 2 == 1)) | ((x == s) & (y % 2 == 1))
        peers += greet_if(core1 & near, [(s, z * 2)])
    peers += greet_if(head, [(0, 5), (0, 13)])
    peers += greet_if((p == 0) & ((q == 5) | (q == 13)), [(0, 0)])
    peers += greet_if((p == 0) & (q == 5), [(0, 9)])
    peers += greet_if((p == 0) & (q == 9), [(0, 5)])
    peers += greet_if(core1 & (y == 0) & (x % 2 == 0), [((x + 2) % 4, q)])
    peers += greet_if(core1 & (y % 2 == 0), [((y + 2) % 4 * 4 + x, q)])

    each_source(lambda s: a_load(s).wait(), lambda g, s: b_load(g, s).wait())
    for s in range(2):
        @pl.when((p == s) & (q == s))
        def _():
            here = slice(s * NB, (s + 1) * NB)
            a_buf[:NB, here] = a_buf[:NB, here] + jnp.where(identity(), noise_ref[:, :NB], 0.0)

    pl.semaphore_wait(barrier, peers)

    def remote(src, dst, send_sem, recv_sem, device):
        return pltpu.make_async_remote_copy(
            src_ref=src, dst_ref=dst, send_sem=send_sem, recv_sem=recv_sem, device_id=device, device_id_type=MESH
        )

    def m_copy(which):
        return remote(a_buf.at[pl.ds(0, NB), half[which]], m_buf.at[which], m_send.at[which], m_recv.at[which], (0, 0))

    for which in range(2):
        @pl.when((p == 1) & (q == which))
        def _():
            m_copy(which).start()

    def a_ring(n, back):
        part = a_buf.at[pl.ds(n * A_ROWS, A_ROWS), :]
        return remote(part, part, a_send.at[back, jnp.where(n < 2 * A_ONE, 0, 1)], a_recv.at[n], (p, z_next[back] * 2))

    def a_sib(first, count):
        part = a_buf.at[pl.ds(first * A_ROWS, count * A_ROWS), :]
        return remote(part, part, s_send, s_recv, sib)

    def a_sent(back, group):
        part = a_buf.at[pl.ds(0, (A_ONE, A_TURN - A_ONE)[group] * A_ROWS), :]
        return remote(part, part, a_send.at[back, group], a_recv.at[0], (p, z_next[back] * 2))

    def a_half(s, n, back):
        part = a_buf.at[pl.ds(n * A_ROWS, A_ROWS), half[s]]
        return remote(part, part, g_send.at[back], (a_recv, o_recv)[s].at[n], (p, z_next[back] * 2))

    def a_gave(s, back):
        part = a_buf.at[pl.ds(0, A_TURN * A_ROWS), half[s]]
        return remote(part, part, g_send.at[back], g_recv, (p, z_next[back] * 2))

    def a_join(s):
        part = a_buf.at[:, half[s]]
        return remote(part, part, g_send.at[2], g_recv, sib)

    def b_half(g, s, n, k):
        part = b_buf.at[s, pl.ds(n * B_ROWS, B_ROWS), side[g]]
        return remote(part, part, g_send.at[3], (r_recv, b_recv)[g].at[s, n], (rows_next[k], z * 2 + 1))

    def b_gave(g, s):
        part = b_buf.at[s, :, side[g]]
        return remote(part, part, g_send.at[3], g_recv, sib)

    def b_plane(s, n, k, way):
        part = b_buf.at[s, pl.ds(n * B_ROWS, B_ROWS), :]
        return remote(part, part, b_send.at[way, s, k], b_recv.at[s, n], (rows_next[way], z * 2 + 1))

    def b_sent(s, k, way):
        part = b_buf.at[s, pl.ds(0, NB // 4), :]
        return remote(part, part, b_send.at[way, s, k], b_recv.at[s, 0], (rows_next[way], z * 2 + 1))

    def b_sib(s, first, count):
        part = b_buf.at[s, pl.ds(first * (NB // 4), count * (NB // 4)), side[0]]
        return remote(part, part, t_send.at[s], t_recv.at[s], sib)

    a_hops = (z, 8 - z)

    def a_chunk(k, back):
        return jnp.where(k < A_ONE, 2 * k + back, A_ONE + k)

    def a_comes(k, back):
        return (k < A_ONE) | (a_hops[back] <= 4 - back)

    def a_more(k, back):
        return jnp.where(k < A_ONE, a_hops[back] < 7, a_hops[back] < 4 - back)

    def tree(s, k):
        dx, dy = (x + 4 - s) % 4, y
        u, v = ((dx, dy), (dy, (4 - dx) % 4), ((4 - dx) % 4, (4 - dy) % 4), ((4 - dy) % 4, dx))[k]
        hops = jnp.where(u == 0, 2, u) + jnp.minimum(v, 4 - v)
        sends = (
            (u == 2) | ((u == 1) & (v < 3)),
            (u == 1) & (v < 2),
            (u == 1) & (v >= 1),
            (v == 0) & ((u == 1) | (u == 2)),
        )
        return hops, [sends[(d - k) % 4] for d in range(4)]

    trees = {(s, k): tree(s, k) for s in range(2) for k in range(4)}
    b_last = []
    for s in range(2):
        last = trees[s, 0][0]
        for k in range(1, 4):
            last = jnp.where(trees[s, k][0] > last, trees[s, k][0], last)
        b_last.append(last)


    def b_first(g, s):
        def step(m, carry):
            for k in range(4):
                b_half(g, s, 4 * m + k, k).start()
            return carry

        lax.fori_loop(0, NBC // 4, step, 0)

    def a_first(s):
        def step(k, carry):
            for back in range(2):
                a_half(s, a_chunk(k, back), back).start()
            return carry

        lax.fori_loop(0, A_TURN, step, 0)
        a_join(s).start()

    each_source(lambda s: None, b_first)
    each_source(a_first, lambda g, s: None)

    top = core1 & (p == 0)
    edge = core1 & (y == 0)
    every, large, strips = range(NF), range(STRIPS), range(STRIPS, NF)
    f_ways = [(head, (0, k), every) for k in (5, 13, 1)]
    f_ways += [(top & (z == 2), (0, 9), strips)] + [(top & (z == 2), (0, k), every) for k in (7, 3)] + [(top & (z == 6), (0, k), every) for k in (11, 15)]
    f_ways += [(top & (z == 5), (0, 9), large)]
    f_ways += [(top, (2, q), strips), (top, (1, q), every), (top, (3, q), every), (edge & (x == 1), (2, q), large)]
    f_ways += [(edge, (8 + x, q), strips), (edge, (4 + x, q), every), (edge, (12 + x, q), every)]
    f_ways += [(core1 & (y == 1), (8 + x, q), large)]
    f_ways += [(core1 & ((p != 0) | (q != 1)), sib, every)]
    F_HEAD = 3

    def f_copy(n, way, device):
        row, size, width = PIECES[n]
        part = f_buf.at[pl.ds(row, size), pl.ds(0, width)]
        if way == len(f_ways) - 1:
            return remote(part, part, f_send.at[way], h_recv, device)
        return remote(part, part, f_send.at[way], f_recv.at[n], device)

    def f_whole(way, pieces):
        part = f_buf.at[pl.ds(0, sum(PIECES[n][1] * PIECES[n][2] for n in pieces) // NB), :]
        return remote(part, part, f_send.at[way], h_recv, sib)


    def pass_f(n):
        f_copy(n, 0, sib).wait_recv()
        for way in range(F_HEAD, len(f_ways)):
            if n in f_ways[way][2]:
                @pl.when(f_ways[way][0])
                def _():
                    f_copy(n, way, f_ways[way][1]).start()

    def far(v):
        return jnp.where(v == 0, 0, jnp.where(v == 2, 2, 1))

    f_slot = F_SLOT + far(x) + far(y) + jnp.where(z == 0, 0, jnp.where(z == 4, 3, jnp.where(z % 4 == 2, 1, 2)))

    def pass_a(slot, carry):
        @pl.when(core0 & (z != 0))
        def _():
            for back in range(2):
                m = slot - HOP * a_hops[back]
                k = (m + 3 * A_TURN) % A_TURN
                n = a_chunk(k, back)

                @pl.when((m >= 0) & (m < A_TURN) & a_comes(k, back))
                def _():
                    @pl.when(a_hops[back] == 1)
                    def _():
                        for s in range(2):
                            a_half(s, n, back).wait_recv()

                    @pl.when(a_hops[back] != 1)
                    def _():
                        a_ring(n, back).wait_recv()

                    @pl.when(a_more(k, back))
                    def _():
                        a_ring(n, back).start()

                    a_sib(n, 1).start()

        return carry

    def pass_b(slot, carry):
        @pl.when(core1)
        def _():
            for (s, k), (hops, sends) in trees.items():
                m = slot - hops
                n = 4 * ((m + NBC) % (NBC // 4)) + k

                @pl.when((p != s) & (m >= 0) & (m < NBC // 4))
                def _():
                    @pl.when(hops == 1)
                    def _():
                        for g in range(2):
                            b_half(g, s, n, k).wait_recv()

                    @pl.when(hops != 1)
                    def _():
                        b_plane(s, n, k, 0).wait_recv()

                    for way in range(4):
                        @pl.when(sends[way])
                        def _():
                            b_plane(s, n, k, way).start()

            for s in range(2):
                m = slot - b_last[s]

                @pl.when((p != s) & (m >= 0) & (m < 4))
                def _():
                    b_sib(s, (m + NBC) % 4, 1).start()

            @pl.when(slot == f_slot)
            def _():
                for n in large:
                    pass_f(n)

        return carry

    lax.fori_loop(0, A_SLOTS, pass_a, 0)
    lax.fori_loop(0, B_SLOTS, pass_b, 0)

    def a_wait_sib():
        @pl.when(a_source)
        def _():
            a_join(0).wait_recv()

        @pl.when(jnp.logical_not(a_source))
        def _():
            a_sib(0, NA).wait_recv()

    def b_wait_sib():
        for s in range(2):
            @pl.when(p != s)
            def _():
                b_sib(s, 0, 4).wait_recv()

    a_store = pltpu.make_async_copy(a_buf, a_out, local.at[0])

    def b_store(g):
        return pltpu.make_async_copy(b_buf.at[:, :, side[g]], b_out, local.at[1])

    f_store = pltpu.make_async_copy(f_buf, f_out, local.at[2])

    @pl.when(head)
    def _():
        eye = jnp.where(identity(), 1.0, 0.0)

        def put(first, last, value):
            f_buf[first:last, :] = value
            for n in range(NF):
                if first <= PIECES[n][0] < last:
                    for way in range(F_HEAD):
                        f_copy(n, way, f_ways[way][1]).start()

        work[:, :NB] = a_buf[:NB, :NB]
        work[:, NB:] = eye
        factor_inverse(work)
        put(0, NB, work[:, NB:])
        m_copy(0).wait_recv()
        l10 = nt(m_buf[0], work[:, NB:])
        put(NB, 2 * NB, l10)
        m_copy(1).wait_recv()
        work[:, :NB] = m_buf[1] - nt(l10, l10)
        work[:, NB:] = eye

        def strip(k):
            last = 32 * (k + 1)
            for start, size, _ in PIECES:
                if start - 2 * NB + size == last:
                    put(start, start + size, work[last - size : last, NB:])

        factor_inverse(work, strip)
        a_wait_sib()
        b_wait_sib()
        a_store.start()
        b_store(0).start()

    @pl.when(core0 & jnp.logical_not(head))
    def _():
        @pl.when(a_source)
        def _():
            a_wait_sib()

        a_store.start()
        b_wait_sib()
        b_store(0).start()
        f_whole(0, every).wait_recv()

    @pl.when(core1)
    def _():
        b_store(1).start()
        for n in strips:
            pass_f(n)

        a_wait_sib()
        a_store.start()

    f_store.start()

    def a_given(s):
        for back in range(2):
            a_gave(s, back).wait_send()
        a_join(s).wait_send()

    each_source(a_given, lambda g, s: b_gave(g, s).wait_send())

    for back in range(2):
        for group, k in enumerate((0, A_ONE)):
            @pl.when(core0 & (z != 0) & a_comes(k, back) & a_more(k, back))
            def _():
                a_sent(back, group).wait_send()

    @pl.when(core0 & (z != 0))
    def _():
        a_sib(0, NA).wait_send()

    for (s, k), (hops, sends) in trees.items():
        for way in range(4):
            @pl.when(core1 & (p != s) & sends[way])
            def _():
                b_sent(s, k, way).wait_send()

    for s in range(2):
        @pl.when(core1 & (p != s))
        def _():
            b_sib(s, 0, 4).wait_send()

    for way, (sends, device, pieces) in enumerate(f_ways):
        @pl.when(sends)
        def _():
            f_whole(way, pieces).wait_send()

    for which in range(2):
        @pl.when((p == 1) & (q == which))
        def _():
            m_copy(which).wait_send()

    a_store.wait()
    for g in range(2):
        @pl.when(c == g)
        def _():
            b_store(g).wait()

    f_store.wait()


def gather(kernel, noise):
    return pl.pallas_call(
        gather_kernel,
        out_shape=(
            jax.ShapeDtypeStruct((LOCAL, 2 * NB), F32),
            jax.ShapeDtypeStruct((2, NB, LOCAL), F32),
            jax.ShapeDtypeStruct((3 * NB, NB), F32),
        ),
        in_specs=[pl.BlockSpec(memory_space=pl.ANY), pl.BlockSpec(memory_space=pltpu.VMEM)],
        out_specs=[pl.BlockSpec(memory_space=pl.ANY)] * 3,
        scratch_shapes=[
            pltpu.VMEM((LOCAL, 2 * NB), F32),
            pltpu.VMEM((2, NB, 2 * LOCAL), F32),
            pltpu.VMEM((3 * NB, NB), F32),
            pltpu.VMEM((2, NB, NB), F32),
            pltpu.VMEM((NB, 2 * NB), F32),
            pltpu.SemaphoreType.DMA((NA,)),
            pltpu.SemaphoreType.DMA((2, 2)),
            pltpu.SemaphoreType.DMA,
            pltpu.SemaphoreType.DMA,
            pltpu.SemaphoreType.DMA((2, NBC)),
            pltpu.SemaphoreType.DMA((4, 2, 4)),
            pltpu.SemaphoreType.DMA((NF,)),
            pltpu.SemaphoreType.DMA((18,)),
            pltpu.SemaphoreType.DMA((2,)),
            pltpu.SemaphoreType.DMA((2,)),
            pltpu.SemaphoreType.DMA,
            pltpu.SemaphoreType.DMA((4,)),
            pltpu.SemaphoreType.DMA((NA,)),
            pltpu.SemaphoreType.DMA((2, NBC)),
            pltpu.SemaphoreType.DMA((2,)),
            pltpu.SemaphoreType.DMA((2,)),
            pltpu.SemaphoreType.DMA,
            pltpu.SemaphoreType.DMA((3,)),
        ],
        compiler_params=pltpu.CompilerParams(
            collective_id=0, has_side_effects=True, vmem_limit_bytes=48 * 2**20
        ),
        name="gather_factor",
    )(kernel, noise)


def split(value):
    high = value.astype(jnp.bfloat16)
    return high, (value - high.astype(F32)).astype(jnp.bfloat16)


def left(parts):
    return jnp.concatenate([parts[0], parts[0], parts[1]], axis=1)


def below(parts):
    return jnp.concatenate([parts[0], parts[1], parts[0]], axis=0)


def beside(parts):
    return jnp.concatenate([parts[0], parts[1], parts[0]], axis=1)


def product(a, b, dims=((1,), (0,))):
    return lax.dot_general(a, b, (dims, ((), ())), preferred_element_type=F32)


NT = ((1,), (1,))


def update_kernel(
    m_ref, noise_ref, a_ref, b_ref, f_ref, out_ref,
    m_buf, a_buf, b_buf, f_buf, rows, cols, m_sem, a_sem, b_sem, f_sem, out_sem, up_sem,
):
    p, q = lax.axis_index("row"), lax.axis_index("col")
    strip = [pl.ds(t * NB, NB) for t in range(T)]
    f_load = pltpu.make_async_copy(f_ref, f_buf, f_sem)
    b_load = pltpu.make_async_copy(b_ref, b_buf, b_sem)
    a_load = pltpu.make_async_copy(a_ref, a_buf, a_sem)
    lower = [(strip[t], pl.ds(0, (t + 1) * NB)) for t in range(T)]
    upper = [(strip[t], pl.ds((t + 1) * NB, LOCAL - (t + 1) * NB)) for t in range(T - 1)]
    m_load = [pltpu.make_async_copy(m_ref.at[lower[t]], m_buf.at[lower[t]], m_sem.at[t]) for t in range(T)]
    store = [pltpu.make_async_copy(m_buf.at[lower[t]], out_ref.at[lower[t]], out_sem.at[t]) for t in range(T)]
    u_load = [pltpu.make_async_copy(m_ref.at[upper[t]], m_buf.at[upper[t]], up_sem.at[0, t]) for t in range(T - 1)]
    u_store = [pltpu.make_async_copy(m_buf.at[upper[t]], out_ref.at[upper[t]], up_sem.at[1, t]) for t in range(T - 1)]
    f_load.start()
    a_load.start()
    b_load.start()
    for copy in u_load + m_load:
        copy.start()

    f_load.wait()
    x0, l10, x1 = [split(f_buf[k * NB : (k + 1) * NB, :]) for k in range(3)]
    a_load.wait()
    row0 = product(left(split(a_buf[:, :NB])), beside(x0), NT)
    row0_parts = split(row0)
    row1 = product(left(split(a_buf[:, NB:] - product(left(row0_parts), beside(l10), NT))), beside(x1), NT)
    row1_parts = split(row1)
    for at, value in enumerate((row0_parts[0], row1_parts[0], row0_parts[1], row1_parts[1])):
        rows[:, at * NB : (at + 1) * NB] = value
    for load, copy in zip(u_load, u_store):
        load.wait()
        copy.start()
    b_load.wait()
    col0 = split(product(left(x0), below(split(b_buf[0]))))
    col1 = split(product(left(x1), below(split(b_buf[1] - product(left(l10), below(col0))))))
    for at, value in enumerate((col0[0], col1[0], col0[1], col1[1])):
        cols[at * NB : (at + 1) * NB, :] = value

    for t in range(T):
        m_load[t].wait()
    i0 = lax.broadcasted_iota(jnp.int32, (NB, NB), 0)
    i1 = lax.broadcasted_iota(jnp.int32, (NB, NB), 1)
    for col in range(T):
        at = slice(col * NB, (col + 1) * NB)

        def blocks():
            high, low = slice(0, 2 * NB), slice(2 * NB, 4 * NB)
            u = jnp.concatenate([rows[col * NB :, high], rows[col * NB :, high], rows[col * NB :, low]], axis=1)
            v = jnp.concatenate([cols[high, at], cols[low, at], cols[high, at]], axis=0)
            value = m_buf[col * NB :, at] - product(u, v)
            first = value[:NB] + jnp.where((i0 == i1) & (p == q), noise_ref[:, at], 0.0)
            m_buf[at, at] = jnp.where(p >= q, first, m_buf[at, at])
            if col < T - 1:
                m_buf[(col + 1) * NB :, at] = value[NB:]

        if col > 0:
            blocks()
        else:
            pl.when(q >= 2)(blocks)

            @pl.when(q < 2)
            def _():
                panel = jnp.where(q == 0, row0, row1)
                first = jnp.where((p == q) & (i0 < i1), 0.0, panel[:NB])
                m_buf[at, at] = jnp.where(p >= q, first, m_buf[at, at])
                m_buf[NB:, at] = panel[NB:]

        store[col].start()
    for copy in store + u_store:
        copy.wait()


def update(kernel, noise, a, b, f):
    whole = pl.BlockSpec(memory_space=pl.ANY)
    return pl.pallas_call(
        update_kernel,
        out_shape=jax.ShapeDtypeStruct((LOCAL, LOCAL), F32),
        in_specs=[whole, pl.BlockSpec(memory_space=pltpu.VMEM), whole, whole, whole],
        out_specs=whole,
        scratch_shapes=[
            pltpu.VMEM((LOCAL, LOCAL), F32),
            pltpu.VMEM((LOCAL, 2 * NB), F32),
            pltpu.VMEM((2, NB, LOCAL), F32),
            pltpu.VMEM((3 * NB, NB), F32),
            pltpu.VMEM((LOCAL, 4 * NB), jnp.bfloat16),
            pltpu.VMEM((4 * NB, LOCAL), jnp.bfloat16),
            pltpu.SemaphoreType.DMA((T,)),
            pltpu.SemaphoreType.DMA,
            pltpu.SemaphoreType.DMA,
            pltpu.SemaphoreType.DMA,
            pltpu.SemaphoreType.DMA((T,)),
            pltpu.SemaphoreType.DMA((2, T - 1)),
        ],
        compiler_params=pltpu.CompilerParams(vmem_limit_bytes=48 * 2**20),
        name="update",
    )(kernel, noise, a, b, f)


def body(kernel, noise):
    noise = noise.reshape(1, LOCAL)
    a, b, f = gather(kernel, noise)
    return update(kernel, noise, a, b, f)


def solution(mesh):
    return jax.shard_map(
        body,
        mesh=mesh,
        in_specs=(P("row", "col"), P("row")),
        out_specs=P("row", "col"),
        check_vma=False,
    )
```

```python
import functools

import jax
import jax.numpy as jnp
from jax import lax
from jax.experimental import pallas as pl
from jax.experimental.pallas import tpu as pltpu
from jax.sharding import PartitionSpec as P

NB = 256
T = 5
LOCAL = NB * T
MESH = pl.DeviceIdType.MESH
HIGHEST = lax.Precision.HIGHEST
HIGH = lax.Precision.HIGH
F32 = jnp.float32

NA = 20
A_ROWS = LOCAL // NA
A_ONE = NA // 4
A_TURN = NA - A_ONE
HOP = 3
A_SLOTS = max(A_ONE + 7 * HOP, A_TURN + 4 * HOP)
NBC = 16
B_ROWS = NB // NBC
F_SLOT = 3
B_SLOTS = max(9, F_SLOT + 8)
PIECES = (
    ((0, 64, 128), (64, 64, 128), (128, 32, 256), (160, 32, 256), (192, 32, 256), (224, 32, 256))
    + tuple((NB + 32 * n, 32, 256) for n in range(8))
    + ((512, 64, 128), (576, 64, 128), (640, 64, 256), (704, 32, 256), (736, 32, 256))
)
STRIPS = 14
NF = len(PIECES)


def dot(a, b, dims, precision=HIGHEST):
    return lax.dot_general(a, b, (dims, ((), ())), precision=precision, preferred_element_type=F32)


def nn(a, b, precision=HIGHEST):
    return dot(a, b, ((1,), (0,)), precision)


def nt(a, b, precision=HIGHEST):
    return dot(a, b, ((1,), (1,)), precision)


def tn(a, b, precision=HIGHEST):
    return dot(a, b, ((0,), (0,)), precision)


def eliminate(rows, first):
    width = rows.shape[1]
    done = []
    for g in range(4):
        n = rows.shape[0]
        sub = lax.broadcasted_iota(jnp.int32, (n, 128), 0)
        at = first + 8 * g
        cols = [jnp.broadcast_to(rows[:, at + c : at + c + 1], (n, 128)) for c in range(8)]
        for j in range(8):
            inv = pltpu.reciprocal(cols[j][j : j + 1, :], approx=True)
            scale = jnp.where(sub > j, cols[j] * inv, 0.0)
            for c in range(j + 1, 8):
                cols[c] = cols[c] - scale * cols[c][j : j + 1, :]
            pivot = rows[j : j + 1, :]
            rows = jnp.concatenate(
                [rows[:, w : w + 128] - scale * pivot[:, w : w + 128] for w in range(0, width, 128)], axis=1
            )
        sub8 = lax.broadcasted_iota(jnp.int32, (8, 128), 0)
        diag = cols[0][:8]
        for j in range(1, 8):
            diag = jnp.where(sub8 == j, cols[j][:8], diag)
        root = lax.rsqrt(diag)
        done.append(rows[:8] * jnp.concatenate([root] * (width // 128), axis=1))
        rows = rows[8:]
    return jnp.concatenate(done, axis=0)


def factor_inverse(work, done=lambda k: None):
    following = None
    for k in range(8):
        r0 = 32 * k
        lo, hi = r0 // 128 * 128, NB + (r0 + 32 + 127) // 128 * 128
        rows = work[r0 : r0 + 32, lo:hi] if following is None else following
        rows = eliminate(rows, r0 - lo)
        work[r0 : r0 + 32, lo:hi] = rows
        done(k)
        if k == 7:
            break
        r1 = r0 + 32
        lo1, hi1 = r1 // 128 * 128, NB + (r1 + 32 + 127) // 128 * 128
        product = tn(rows[:, r1 - lo : r1 - lo + 32], rows)
        if hi1 > hi:
            product = jnp.concatenate([product, jnp.zeros((32, hi1 - hi), F32)], axis=1)
        following = work[r1 : r1 + 32, lo1:hi1] - product[:, lo1 - lo :]
        if k < 6:
            r2 = r1 + 32
            lo2 = r2 // 128 * 128
            product = tn(rows[:, lo2 - lo : NB - lo], rows[:, lo2 - lo :])
            work[r2:NB, lo2:hi] = work[r2:NB, lo2:hi] - product[r2 - lo2 :, :]


def identity():
    i0 = lax.broadcasted_iota(jnp.int32, (NB, NB), 0)
    i1 = lax.broadcasted_iota(jnp.int32, (NB, NB), 1)
    return i0 == i1


def gather_kernel(
    kernel_ref, noise_ref, a_out, b_out, f_out,
    a_buf, b_buf, f_buf, m_buf, work,
    a_recv, a_send, s_recv, s_send, b_recv, b_send, f_recv, f_send, m_recv, m_send, g_recv, g_send, o_recv, r_recv, t_recv, t_send, h_recv, local,
):
    p, q = lax.axis_index("row"), lax.axis_index("col")
    y, x, z, c = p // 4, p % 4, q // 2, q % 2
    rows_next = (y * 4 + (x + 1) % 4, (y + 1) % 4 * 4 + x, y * 4 + (x + 3) % 4, (y + 3) % 4 * 4 + x)
    z_next = ((z + 1) % 8, (z + 7) % 8)
    sib = (p, z * 2 + 1 - c)
    core0, core1 = c == 0, c == 1
    head = (p == 0) & (q == 0)
    a_source, b_source = z == 0, p < 2

    half = [pl.ds(k * NB, NB) for k in range(2)]
    side = [pl.ds(k * LOCAL, LOCAL) for k in range(2)]

    def a_load(s):
        return pltpu.make_async_copy(kernel_ref.at[:, pl.ds(0, NB)], a_buf.at[:, half[s]], local.at[0])

    def b_load(g, s):
        return pltpu.make_async_copy(kernel_ref.at[pl.ds(0, NB), :], b_buf.at[s, :, side[g]], local.at[1])

    def each_source(run_a, run_b):
        for s in range(2):
            @pl.when(a_source & (c == s))
            def _():
                run_a(s)

            for g in range(2):
                @pl.when((p == s) & (c == g))
                def _():
                    run_b(g, s)

    each_source(lambda s: a_load(s).start(), lambda g, s: b_load(g, s).start())
    for row in (0, 2 * NB):
        f_buf[row : row + 128, 128:] = jnp.zeros((128, 128), F32)

    barrier = pltpu.get_barrier_semaphore()
    peers = jnp.int32(7)

    def greet(device):
        pl.semaphore_signal(barrier, inc=1, device_id=device, device_id_type=MESH)

    for row in rows_next:
        greet((row, q))
    for level in z_next:
        greet((p, level * 2 + c))
    greet(sib)

    def greet_if(condition, devices):
        @pl.when(condition)
        def _():
            for device in devices:
                greet(device)

        return jnp.where(condition, len(devices), 0)

    peers += greet_if(a_source & core1, [(p, 2), (p, 14)])
    peers += greet_if(core0 & ((z == 1) | (z == 7)), [(p, 1)])
    peers += greet_if(b_source & core0, [(row, z * 2 + 1) for row in rows_next])
    for s in range(2):
        near = ((y == 0) & ((x + 4 - s) % 2 == 1)) | ((x == s) & (y % 2 == 1))
        peers += greet_if(core1 & near, [(s, z * 2)])
    peers += greet_if(head, [(0, 5), (0, 13)])
    peers += greet_if((p == 0) & ((q == 5) | (q == 13)), [(0, 0)])
    peers += greet_if((p == 0) & (q == 5), [(0, 9)])
    peers += greet_if((p == 0) & (q == 9), [(0, 5)])
    peers += greet_if(core1 & (y == 0) & (x % 2 == 0), [((x + 2) % 4, q)])
    peers += greet_if(core1 & (y % 2 == 0), [((y + 2) % 4 * 4 + x, q)])

    each_source(lambda s: a_load(s).wait(), lambda g, s: b_load(g, s).wait())
    for s in range(2):
        @pl.when((p == s) & (q == s))
        def _():
            here = slice(s * NB, (s + 1) * NB)
            a_buf[:NB, here] = a_buf[:NB, here] + jnp.where(identity(), noise_ref[:, :NB], 0.0)

    pl.semaphore_wait(barrier, peers)

    def remote(src, dst, send_sem, recv_sem, device):
        return pltpu.make_async_remote_copy(
            src_ref=src, dst_ref=dst, send_sem=send_sem, recv_sem=recv_sem, device_id=device, device_id_type=MESH
        )

    def m_copy(which):
        return remote(a_buf.at[pl.ds(0, NB), half[which]], m_buf.at[which], m_send.at[which], m_recv.at[which], (0, 0))

    for which in range(2):
        @pl.when((p == 1) & (q == which))
        def _():
            m_copy(which).start()

    def a_ring(n, back):
        part = a_buf.at[pl.ds(n * A_ROWS, A_ROWS), :]
        return remote(part, part, a_send.at[back, jnp.where(n < 2 * A_ONE, 0, 1)], a_recv.at[n], (p, z_next[back] * 2))

    def a_sib(first, count):
        part = a_buf.at[pl.ds(first * A_ROWS, count * A_ROWS), :]
        return remote(part, part, s_send, s_recv, sib)

    def a_sent(back, group):
        part = a_buf.at[pl.ds(0, (A_ONE, A_TURN - A_ONE)[group] * A_ROWS), :]
        return remote(part, part, a_send.at[back, group], a_recv.at[0], (p, z_next[back] * 2))

    def a_half(s, n, back):
        part = a_buf.at[pl.ds(n * A_ROWS, A_ROWS), half[s]]
        return remote(part, part, g_send.at[back], (a_recv, o_recv)[s].at[n], (p, z_next[back] * 2))

    def a_gave(s, back):
        part = a_buf.at[pl.ds(0, A_TURN * A_ROWS), half[s]]
        return remote(part, part, g_send.at[back], g_recv, (p, z_next[back] * 2))

    def a_join(s):
        part = a_buf.at[:, half[s]]
        return remote(part, part, g_send.at[2], g_recv, sib)

    def b_half(g, s, n, k):
        part = b_buf.at[s, pl.ds(n * B_ROWS, B_ROWS), side[g]]
        return remote(part, part, g_send.at[3], (r_recv, b_recv)[g].at[s, n], (rows_next[k], z * 2 + 1))

    def b_gave(g, s):
        part = b_buf.at[s, :, side[g]]
        return remote(part, part, g_send.at[3], g_recv, sib)

    def b_plane(s, n, k, way):
        part = b_buf.at[s, pl.ds(n * B_ROWS, B_ROWS), :]
        return remote(part, part, b_send.at[way, s, k], b_recv.at[s, n], (rows_next[way], z * 2 + 1))

    def b_sent(s, k, way):
        part = b_buf.at[s, pl.ds(0, NB // 4), :]
        return remote(part, part, b_send.at[way, s, k], b_recv.at[s, 0], (rows_next[way], z * 2 + 1))

    def b_sib(s, first, count):
        part = b_buf.at[s, pl.ds(first * (NB // 4), count * (NB // 4)), side[0]]
        return remote(part, part, t_send.at[s], t_recv.at[s], sib)

    a_hops = (z, 8 - z)

    def a_chunk(k, back):
        return jnp.where(k < A_ONE, 2 * k + back, A_ONE + k)

    def a_comes(k, back):
        return (k < A_ONE) | (a_hops[back] <= 4 - back)

    def a_more(k, back):
        return jnp.where(k < A_ONE, a_hops[back] < 7, a_hops[back] < 4 - back)

    def tree(s, k):
        dx, dy = (x + 4 - s) % 4, y
        u, v = ((dx, dy), (dy, (4 - dx) % 4), ((4 - dx) % 4, (4 - dy) % 4), ((4 - dy) % 4, dx))[k]
        hops = jnp.where(u == 0, 2, u) + jnp.minimum(v, 4 - v)
        sends = (
            (u == 2) | ((u == 1) & (v < 3)),
            (u == 1) & (v < 2),
            (u == 1) & (v >= 1),
            (v == 0) & ((u == 1) | (u == 2)),
        )
        return hops, [sends[(d - k) % 4] for d in range(4)]

    trees = {(s, k): tree(s, k) for s in range(2) for k in range(4)}
    b_last = []
    for s in range(2):
        last = trees[s, 0][0]
        for k in range(1, 4):
            last = jnp.where(trees[s, k][0] > last, trees[s, k][0], last)
        b_last.append(last)


    def b_first(g, s):
        def step(m, carry):
            for k in range(4):
                b_half(g, s, 4 * m + k, k).start()
            return carry

        lax.fori_loop(0, NBC // 4, step, 0)

    def a_first(s):
        def step(k, carry):
            for back in range(2):
                a_half(s, a_chunk(k, back), back).start()
            return carry

        lax.fori_loop(0, A_TURN, step, 0)
        a_join(s).start()

    each_source(lambda s: None, b_first)
    each_source(a_first, lambda g, s: None)

    top = core1 & (p == 0)
    edge = core1 & (y == 0)
    every, large, strips = range(NF), range(STRIPS), range(STRIPS, NF)
    f_ways = [(head, (0, k), every) for k in (5, 13, 1)]
    f_ways += [(top & (z == 2), (0, 9), strips)] + [(top & (z == 2), (0, k), every) for k in (7, 3)] + [(top & (z == 6), (0, k), every) for k in (11, 15)]
    f_ways += [(top & (z == 5), (0, 9), large)]
    f_ways += [(top, (2, q), strips), (top, (1, q), every), (top, (3, q), every), (edge & (x == 1), (2, q), large)]
    f_ways += [(edge, (8 + x, q), strips), (edge, (4 + x, q), every), (edge, (12 + x, q), every)]
    f_ways += [(core1 & (y == 1), (8 + x, q), large)]
    f_ways += [(core1 & ((p != 0) | (q != 1)), sib, every)]
    F_HEAD = 3

    def f_copy(n, way, device):
        row, size, width = PIECES[n]
        part = f_buf.at[pl.ds(row, size), pl.ds(0, width)]
        if way == len(f_ways) - 1:
            return remote(part, part, f_send.at[way], h_recv, device)
        return remote(part, part, f_send.at[way], f_recv.at[n], device)

    def f_whole(way, pieces):
        part = f_buf.at[pl.ds(0, sum(PIECES[n][1] * PIECES[n][2] for n in pieces) // NB), :]
        return remote(part, part, f_send.at[way], h_recv, sib)


    def pass_f(n):
        f_copy(n, 0, sib).wait_recv()
        for way in range(F_HEAD, len(f_ways)):
            if n in f_ways[way][2]:
                @pl.when(f_ways[way][0])
                def _():
                    f_copy(n, way, f_ways[way][1]).start()

    def far(v):
        return jnp.where(v == 0, 0, jnp.where(v == 2, 2, 1))

    f_slot = F_SLOT + far(x) + far(y) + jnp.where(z == 0, 0, jnp.where(z == 4, 3, jnp.where(z % 4 == 2, 1, 2)))

    def pass_a(slot, carry):
        @pl.when(core0 & (z != 0))
        def _():
            for back in range(2):
                m = slot - HOP * a_hops[back]
                k = (m + 3 * A_TURN) % A_TURN
                n = a_chunk(k, back)

                @pl.when((m >= 0) & (m < A_TURN) & a_comes(k, back))
                def _():
                    @pl.when(a_hops[back] == 1)
                    def _():
                        for s in range(2):
                            a_half(s, n, back).wait_recv()

                    @pl.when(a_hops[back] != 1)
                    def _():
                        a_ring(n, back).wait_recv()

                    @pl.when(a_more(k, back))
                    def _():
                        a_ring(n, back).start()

                    a_sib(n, 1).start()

        return carry

    def pass_b(slot, carry):
        @pl.when(core1)
        def _():
            for (s, k), (hops, sends) in trees.items():
                m = slot - hops
                n = 4 * ((m + NBC) % (NBC // 4)) + k

                @pl.when((p != s) & (m >= 0) & (m < NBC // 4))
                def _():
                    @pl.when(hops == 1)
                    def _():
                        for g in range(2):
                            b_half(g, s, n, k).wait_recv()

                    @pl.when(hops != 1)
                    def _():
                        b_plane(s, n, k, 0).wait_recv()

                    for way in range(4):
                        @pl.when(sends[way])
                        def _():
                            b_plane(s, n, k, way).start()

            for s in range(2):
                m = slot - b_last[s]

                @pl.when((p != s) & (m >= 0) & (m < 4))
                def _():
                    b_sib(s, (m + NBC) % 4, 1).start()

            @pl.when(slot == f_slot)
            def _():
                for n in large:
                    pass_f(n)

        return carry

    lax.fori_loop(0, A_SLOTS, pass_a, 0)
    lax.fori_loop(0, B_SLOTS, pass_b, 0)

    def a_wait_sib():
        @pl.when(a_source)
        def _():
            a_join(0).wait_recv()

        @pl.when(jnp.logical_not(a_source))
        def _():
            a_sib(0, NA).wait_recv()

    def b_wait_sib():
        for s in range(2):
            @pl.when(p != s)
            def _():
                b_sib(s, 0, 4).wait_recv()

    a_store = pltpu.make_async_copy(a_buf, a_out, local.at[0])

    def b_store(g):
        return pltpu.make_async_copy(b_buf.at[:, :, side[g]], b_out, local.at[1])

    f_store = pltpu.make_async_copy(f_buf, f_out, local.at[2])

    @pl.when(head)
    def _():
        eye = jnp.where(identity(), 1.0, 0.0)

        def put(first, last, value):
            f_buf[first:last, :] = value
            for n in range(NF):
                if first <= PIECES[n][0] < last:
                    for way in range(F_HEAD):
                        f_copy(n, way, f_ways[way][1]).start()

        work[:, :NB] = a_buf[:NB, :NB]
        work[:, NB:] = eye
        factor_inverse(work)
        put(0, NB, work[:, NB:])
        m_copy(0).wait_recv()
        l10 = nt(m_buf[0], work[:, NB:])
        put(NB, 2 * NB, l10)
        m_copy(1).wait_recv()
        work[:, :NB] = m_buf[1] - nt(l10, l10)
        work[:, NB:] = eye

        def strip(k):
            last = 32 * (k + 1)
            for start, size, _ in PIECES:
                if start - 2 * NB + size == last:
                    put(start, start + size, work[last - size : last, NB:])

        factor_inverse(work, strip)
        a_wait_sib()
        b_wait_sib()
        a_store.start()
        b_store(0).start()

    @pl.when(core0 & jnp.logical_not(head))
    def _():
        @pl.when(a_source)
        def _():
            a_wait_sib()

        a_store.start()
        b_wait_sib()
        b_store(0).start()
        f_whole(0, every).wait_recv()

    @pl.when(core1)
    def _():
        b_store(1).start()
        for n in strips:
            pass_f(n)

        a_wait_sib()
        a_store.start()

    f_store.start()

    def a_given(s):
        for back in range(2):
            a_gave(s, back).wait_send()
        a_join(s).wait_send()

    each_source(a_given, lambda g, s: b_gave(g, s).wait_send())

    for back in range(2):
        for group, k in enumerate((0, A_ONE)):
            @pl.when(core0 & (z != 0) & a_comes(k, back) & a_more(k, back))
            def _():
                a_sent(back, group).wait_send()

    @pl.when(core0 & (z != 0))
    def _():
        a_sib(0, NA).wait_send()

    for (s, k), (hops, sends) in trees.items():
        for way in range(4):
            @pl.when(core1 & (p != s) & sends[way])
            def _():
                b_sent(s, k, way).wait_send()

    for s in range(2):
        @pl.when(core1 & (p != s))
        def _():
            b_sib(s, 0, 4).wait_send()

    for way, (sends, device, pieces) in enumerate(f_ways):
        @pl.when(sends)
        def _():
            f_whole(way, pieces).wait_send()

    for which in range(2):
        @pl.when((p == 1) & (q == which))
        def _():
            m_copy(which).wait_send()

    a_store.wait()
    for g in range(2):
        @pl.when(c == g)
        def _():
            b_store(g).wait()

    f_store.wait()


def gather(kernel, noise):
    return pl.pallas_call(
        gather_kernel,
        out_shape=(
            jax.ShapeDtypeStruct((LOCAL, 2 * NB), F32),
            jax.ShapeDtypeStruct((2, NB, LOCAL), F32),
            jax.ShapeDtypeStruct((3 * NB, NB), F32),
        ),
        in_specs=[pl.BlockSpec(memory_space=pl.ANY), pl.BlockSpec(memory_space=pltpu.VMEM)],
        out_specs=[pl.BlockSpec(memory_space=pl.ANY)] * 3,
        scratch_shapes=[
            pltpu.VMEM((LOCAL, 2 * NB), F32),
            pltpu.VMEM((2, NB, 2 * LOCAL), F32),
            pltpu.VMEM((3 * NB, NB), F32),
            pltpu.VMEM((2, NB, NB), F32),
            pltpu.VMEM((NB, 2 * NB), F32),
            pltpu.SemaphoreType.DMA((NA,)),
            pltpu.SemaphoreType.DMA((2, 2)),
            pltpu.SemaphoreType.DMA,
            pltpu.SemaphoreType.DMA,
            pltpu.SemaphoreType.DMA((2, NBC)),
            pltpu.SemaphoreType.DMA((4, 2, 4)),
            pltpu.SemaphoreType.DMA((NF,)),
            pltpu.SemaphoreType.DMA((18,)),
            pltpu.SemaphoreType.DMA((2,)),
            pltpu.SemaphoreType.DMA((2,)),
            pltpu.SemaphoreType.DMA,
            pltpu.SemaphoreType.DMA((4,)),
            pltpu.SemaphoreType.DMA((NA,)),
            pltpu.SemaphoreType.DMA((2, NBC)),
            pltpu.SemaphoreType.DMA((2,)),
            pltpu.SemaphoreType.DMA((2,)),
            pltpu.SemaphoreType.DMA,
            pltpu.SemaphoreType.DMA((3,)),
        ],
        compiler_params=pltpu.CompilerParams(
            collective_id=0, has_side_effects=True, vmem_limit_bytes=48 * 2**20
        ),
        name="gather_factor",
    )(kernel, noise)


def split(value):
    high = value.astype(jnp.bfloat16)
    return high, (value - high.astype(F32)).astype(jnp.bfloat16)


def left(parts):
    return jnp.concatenate([parts[0], parts[0], parts[1]], axis=1)


def below(parts):
    return jnp.concatenate([parts[0], parts[1], parts[0]], axis=0)


def beside(parts):
    return jnp.concatenate([parts[0], parts[1], parts[0]], axis=1)


def product(a, b, dims=((1,), (0,))):
    return lax.dot_general(a, b, (dims, ((), ())), preferred_element_type=F32)


NT = ((1,), (1,))


def update_kernel(
    m_ref, noise_ref, a_ref, b_ref, f_ref, out_ref,
    m_buf, a_buf, b_buf, f_buf, rows, cols, m_sem, a_sem, b_sem, f_sem, out_sem, up_sem,
):
    p, q = lax.axis_index("row"), lax.axis_index("col")
    strip = [pl.ds(t * NB, NB) for t in range(T)]
    f_load = pltpu.make_async_copy(f_ref, f_buf, f_sem)
    b_load = pltpu.make_async_copy(b_ref, b_buf, b_sem)
    a_load = pltpu.make_async_copy(a_ref, a_buf, a_sem)
    lower = [(strip[t], pl.ds(0, (t + 1) * NB)) for t in range(T)]
    upper = [(strip[t], pl.ds((t + 1) * NB, LOCAL - (t + 1) * NB)) for t in range(T - 1)]
    m_load = [pltpu.make_async_copy(m_ref.at[lower[t]], m_buf.at[lower[t]], m_sem.at[t]) for t in range(T)]
    store = [pltpu.make_async_copy(m_buf.at[lower[t]], out_ref.at[lower[t]], out_sem.at[t]) for t in range(T)]
    u_load = [pltpu.make_async_copy(m_ref.at[upper[t]], m_buf.at[upper[t]], up_sem.at[0, t]) for t in range(T - 1)]
    u_store = [pltpu.make_async_copy(m_buf.at[upper[t]], out_ref.at[upper[t]], up_sem.at[1, t]) for t in range(T - 1)]
    f_load.start()
    a_load.start()
    b_load.start()
    for copy in u_load + m_load:
        copy.start()

    f_load.wait()
    x0, l10, x1 = [split(f_buf[k * NB : (k + 1) * NB, :]) for k in range(3)]
    a_load.wait()
    row0 = product(left(split(a_buf[:, :NB])), beside(x0), NT)
    row0_parts = split(row0)
    row1 = product(left(split(a_buf[:, NB:] - product(left(row0_parts), beside(l10), NT))), beside(x1), NT)
    row1_parts = split(row1)
    for at, value in enumerate((row0_parts[0], row1_parts[0], row0_parts[1], row1_parts[1])):
        rows[:, at * NB : (at + 1) * NB] = value
    for load, copy in zip(u_load, u_store):
        load.wait()
        copy.start()
    b_load.wait()
    col0 = split(product(left(x0), below(split(b_buf[0]))))
    col1 = split(product(left(x1), below(split(b_buf[1] - product(left(l10), below(col0))))))
    for at, value in enumerate((col0[0], col1[0], col0[1], col1[1])):
        cols[at * NB : (at + 1) * NB, :] = value

    for t in range(T):
        m_load[t].wait()
    i0 = lax.broadcasted_iota(jnp.int32, (NB, NB), 0)
    i1 = lax.broadcasted_iota(jnp.int32, (NB, NB), 1)
    for col in range(T):
        at = slice(col * NB, (col + 1) * NB)

        def blocks():
            high, low = slice(0, 2 * NB), slice(2 * NB, 4 * NB)
            u = jnp.concatenate([rows[col * NB :, high], rows[col * NB :, high], rows[col * NB :, low]], axis=1)
            v = jnp.concatenate([cols[high, at], cols[low, at], cols[high, at]], axis=0)
            value = m_buf[col * NB :, at] - product(u, v)
            first = value[:NB] + jnp.where((i0 == i1) & (p == q), noise_ref[:, at], 0.0)
            m_buf[at, at] = jnp.where(p >= q, first, m_buf[at, at])
            if col < T - 1:
                m_buf[(col + 1) * NB :, at] = value[NB:]

        if col > 0:
            blocks()
        else:
            pl.when(q >= 2)(blocks)

            @pl.when(q < 2)
            def _():
                panel = jnp.where(q == 0, row0, row1)
                first = jnp.where((p == q) & (i0 < i1), 0.0, panel[:NB])
                m_buf[at, at] = jnp.where(p >= q, first, m_buf[at, at])
                m_buf[NB:, at] = panel[NB:]

        store[col].start()
    for copy in store + u_store:
        copy.wait()


def update(kernel, noise, a, b, f):
    whole = pl.BlockSpec(memory_space=pl.ANY)
    return pl.pallas_call(
        update_kernel,
        out_shape=jax.ShapeDtypeStruct((LOCAL, LOCAL), F32),
        in_specs=[whole, pl.BlockSpec(memory_space=pltpu.VMEM), whole, whole, whole],
        out_specs=whole,
        scratch_shapes=[
            pltpu.VMEM((LOCAL, LOCAL), F32),
            pltpu.VMEM((LOCAL, 2 * NB), F32),
            pltpu.VMEM((2, NB, LOCAL), F32),
            pltpu.VMEM((3 * NB, NB), F32),
            pltpu.VMEM((LOCAL, 4 * NB), jnp.bfloat16),
            pltpu.VMEM((4 * NB, LOCAL), jnp.bfloat16),
            pltpu.SemaphoreType.DMA((T,)),
            pltpu.SemaphoreType.DMA,
            pltpu.SemaphoreType.DMA,
            pltpu.SemaphoreType.DMA,
            pltpu.SemaphoreType.DMA((T,)),
            pltpu.SemaphoreType.DMA((2, T - 1)),
        ],
        compiler_params=pltpu.CompilerParams(vmem_limit_bytes=48 * 2**20),
        name="update",
    )(kernel, noise, a, b, f)


def body(kernel, noise):
    noise = noise.reshape(1, LOCAL)
    a, b, f = gather(kernel, noise)
    return update(kernel, noise, a, b, f)


def solution(mesh):
    return jax.shard_map(
        body,
        mesh=mesh,
        in_specs=(P("row", "col"), P("row")),
        out_specs=P("row", "col"),
        check_vma=False,
    )
```
